512 devices in a mesh: ctx: 64 (over y, z_hi, core), kvh: 8 (over x, z_lo).
Axes of the slice: x: 4, y: 8, z: 8 (z_hi: 4, z_lo: 2; z = z_hi * 2 + z_lo), core: 2. Of those that a mesh axis runs over, the one named last changes fastest.
Arguments:
- queries: bfloat16 [16384, 40, 128], P('ctx', 'kvh'), may hold values from -8 to 8
- key_rows: bfloat16 [16384, 8, 128], P('ctx', 'kvh'), may hold values from -8 to 8
- value_rows: bfloat16 [16384, 8, 128], P('ctx', 'kvh'), may hold values from -6 to 6
- vertical: int32 [8, 16], P('kvh'), may hold values from 0 to 127, as said below
- slash_offsets: int32 [8, 8], P('kvh'), may hold values from 0 to 15, as said below
Outputs:
- attended: bfloat16 [16384, 40, 128], P('ctx', 'kvh')
- profile: float32 [16384], P('ctx')
The draws below stay inside these ranges and needn't reach their ends.
Inputs may be any that keep to these rules, and one draw needn't show every extreme that they name: `vertical`: each row names 16 different key blocks; the first is block 0. `slash_offsets`: each row names 8 different offsets; 0, 1 and 15 are always among them.
All inputs are finite; a program needn't handle non-finite values.
Results may differ from the reference program's by a relative error of at most 0.0075.
Values may be sent and summed in bfloat16 or wider, within the bound.
No kernel may reach another device: no remote copies, remote signals or barrier semaphores. Data moves between devices by JAX's collectives and lax.ppermute only.
A program may use at most 64 MiB of HBM per device.

```python
import math
import jax
import jax.numpy as jnp
from jax import lax

KVH = 8
GROUP = 5
HD = 128
BLK = 128
LAST = 64
NV = 16
NS = 8
HEADS = 40
SEQ = 16384
NBLK = 128
REACH = 16


def draw_queries(key, part):
    key = jax.random.fold_in(key, 1)
    drawn = jnp.clip(jax.random.normal(key, (SEQ, HEADS, HD), jnp.float32), -8.0, 8.0)
    return drawn.astype(jnp.bfloat16)


def draw_key_rows(key, part):
    key = jax.random.fold_in(key, 2)
    drawn = jnp.clip(jax.random.normal(key, (SEQ, KVH, HD), jnp.float32), -8.0, 8.0)
    return drawn.astype(jnp.bfloat16)


def draw_vertical(key, part):
    key = jax.random.fold_in(key, 3)
    head_keys = jax.random.split(key, KVH)
    picks = jax.vmap(lambda one_key: jax.random.permutation(one_key, NBLK - 2)[:NV - 2] + 1)(head_keys)
    first_part = jnp.broadcast_to(jnp.array([0, NBLK - 1], jnp.int32)[None, :], (KVH, 2))
    return jnp.concatenate([first_part, picks.astype(jnp.int32)], axis=1)


def draw_slash_offsets(key, part):
    key = jax.random.fold_in(key, 4)
    head_keys = jax.random.split(key, KVH)
    picks = jax.vmap(lambda one_key: jax.random.permutation(one_key, REACH - 3)[:NS - 3] + 2)(head_keys)
    fixed_part = jnp.broadcast_to(jnp.array([0, 1, REACH - 1], jnp.int32)[None, :], (KVH, 3))
    return jnp.concatenate([fixed_part, picks.astype(jnp.int32)], axis=1)


def level_of(rng, shape, cuts, low, high):
    def one(dim, blocks):
        steps = jax.random.uniform(jax.random.fold_in(jax.random.fold_in(rng, 6), dim), (blocks,), jnp.float32, low / len(cuts), high / len(cuts))
        return jnp.repeat(jnp.exp(steps), shape[dim] // blocks).reshape((-1,) + (1,) * (len(shape) - dim - 1))

    gain = one(*cuts[0])
    for cut in cuts[1:]:
        gain = gain * one(*cut)
    return gain


def noise(key, shape, deviation, bound, shards=(), kind=jnp.bfloat16):
    values = deviation * jax.random.normal(key, shape, jnp.float32)
    if shards:
        values = values * level_of(key, shape, shards, -0.22, 0.18)
    return jnp.clip(values, -bound, bound).astype(kind)


def setup_inputs(seed: int = 0) -> dict:
    arg_keys = jax.random.split(jax.random.key(seed), 6)
    queries = draw_queries(jax.random.fold_in(arg_keys[5], 71), 0)
    key_rows = draw_key_rows(jax.random.fold_in(arg_keys[5], 71), 0)
    value_rows = noise(arg_keys[2], (SEQ, KVH, HD), 1.0, 6.0, ((0, 64), (1, 8)))
    vertical = draw_vertical(jax.random.fold_in(arg_keys[5], 71), 0)
    slash_offsets = draw_slash_offsets(jax.random.fold_in(arg_keys[5], 71), 0)
    return dict(queries=queries, key_rows=key_rows, value_rows=value_rows, vertical=vertical, slash_offsets=slash_offsets)


floor_score = -1e+30

def head_attention(q_head, k_head, v_head, vert_row, slash_row):
    k_blocks = k_head.reshape(NBLK, BLK, HD)
    v_blocks = v_head.reshape(NBLK, BLK, HD)
    q_blocks = q_head.reshape(NBLK, BLK, GROUP, HD)
    slot_index = jnp.arange(NV + NS, dtype=jnp.int32)
    inside = jnp.arange(BLK, dtype=jnp.int32)

    def per_block(packed):
        block_id, q_block = packed
        chosen = jnp.concatenate([vert_row, block_id - slash_row]).astype(jnp.int32)
        in_range = (chosen >= 0) & (chosen <= block_id)
        repeated = (chosen[:, None] == chosen[None, :]) & in_range[None, :] & (slot_index[None, :] < slot_index[:, None])
        usable = in_range & jnp.logical_not(jnp.any(repeated, axis=1))
        clipped = jnp.clip(chosen, 0, NBLK - 1).astype(jnp.int32)
        keys_sel = k_blocks[clipped].reshape(-1, HD).astype(jnp.float32)
        vals_sel = v_blocks[clipped].reshape(-1, HD).astype(jnp.float32)
        scores = jnp.einsum('qgd,kd->gqk', q_block.astype(jnp.float32), keys_sel) / math.sqrt(HD)
        key_pos = (clipped[:, None] * BLK + inside[None, :]).reshape(-1)
        query_pos = block_id * BLK + inside
        allowed = jnp.repeat(usable, BLK)[None, :] & (key_pos[None, :] <= query_pos[:, None])
        scores = jnp.where(allowed[None], scores, floor_score)
        top = lax.optimization_barrier(jnp.max(scores, axis=-1, keepdims=True))
        weights = jnp.where(allowed[None], jnp.exp(scores - top), 0.0)
        total = lax.optimization_barrier(jnp.sum(weights, axis=-1))
        rounded = lax.optimization_barrier(weights.astype(jnp.bfloat16))
        mixed = jnp.einsum('gqk,kd->qgd', rounded.astype(jnp.float32), vals_sel)
        return (mixed / jnp.transpose(total)[:, :, None]).astype(jnp.bfloat16)
    result = lax.map(per_block, (jnp.arange(NBLK, dtype=jnp.int32), q_blocks))
    return result.reshape(SEQ, GROUP, HD)

def estimate(queries, key_rows):
    last_rows = queries[SEQ - LAST:].astype(jnp.float32)
    key_pos = jnp.arange(SEQ, dtype=jnp.int32)
    query_pos = SEQ - LAST + jnp.arange(LAST, dtype=jnp.int32)
    allowed = key_pos[None, :] <= query_pos[:, None]
    profile = jnp.zeros((SEQ,), jnp.float32)
    for kv_head in range(KVH):
        q_group = last_rows[:, kv_head * GROUP:(kv_head + 1) * GROUP]
        scores = jnp.einsum('qgd,kd->gqk', q_group, key_rows[:, kv_head].astype(jnp.float32)) / math.sqrt(HD)
        scores = jnp.where(allowed[None], scores, floor_score)
        top = lax.optimization_barrier(jnp.max(scores, axis=-1, keepdims=True))
        weights = jnp.where(allowed[None], jnp.exp(scores - top), 0.0)
        total = lax.optimization_barrier(jnp.sum(weights, axis=-1, keepdims=True))
        profile = profile + lax.optimization_barrier(jnp.sum(weights / total, axis=(0, 1)))
    return profile * (SEQ / LAST / HEADS)

def reference(queries, key_rows, value_rows, vertical, slash_offsets):
    outputs = []
    for kv_head in range(KVH):
        outputs.append(head_attention(queries[:, kv_head * GROUP:(kv_head + 1) * GROUP], key_rows[:, kv_head], value_rows[:, kv_head], vertical[kv_head], slash_offsets[kv_head]))
    attended = jnp.concatenate(outputs, axis=1)
    profile = estimate(queries, key_rows)
    return (attended, profile)
```

```python
import math

import jax
import jax.numpy as jnp
from jax import lax
from jax.experimental import pallas as pl
from jax.experimental.pallas import tpu as pltpu
from jax.sharding import Mesh
from jax.sharding import PartitionSpec as P

BLK = 128
LAST = 64
NV = 16
NS = 8
HEADS = 40
HD = 128
GROUP = 5
FAR = -1e30
LOG2E = math.log2(math.e)
C = ("zh", "core")
CTX = ("y", "zh", "core")


def spread(x, axis, n):
    return lax.all_to_all(jnp.broadcast_to(x, (n,) + x.shape), axis, 0, 0)


def estimate(q_t, key_rows, position, local, ny, nz):
    rows = GROUP * LAST
    total_len = local * ny * nz * 2
    scale = 1.0 / math.sqrt(HD)
    last = q_t[:, local - LAST :].reshape(ny, rows // ny, HD)
    part = lax.all_to_all(last, "y", 0, 0)[ny - 1]
    part = spread(part, C, 2 * nz)[2 * nz - 1]
    q_last = spread(part, "y", ny).reshape(rows, HD)
    scores = lax.dot_general(q_last, key_rows, (((1,), (1,)), ((), ())), preferred_element_type=jnp.float32) * scale
    key_pos = position * local + jnp.arange(local, dtype=jnp.int32)
    last_pos = total_len - LAST + jnp.arange(rows, dtype=jnp.int32) % LAST
    scores = jnp.where(key_pos[None, :] <= last_pos[:, None], scores, FAR)
    top = jnp.max(scores, axis=-1)
    total = jnp.sum(jnp.exp(scores - top[:, None]), axis=-1)
    both = lax.all_gather(jnp.stack([top, total]), "core")
    core = lax.axis_index("core")
    both = lax.dynamic_slice_in_dim(both.reshape(2, 2, 2, rows // 2), core, 1, 2)[:, :, 0]
    top = jnp.max(both[:, 0], axis=0)
    total = jnp.sum(both[:, 1] * jnp.exp(both[:, 0] - top), axis=0)
    every = spread(jnp.stack([top, total]), ("y", "zh"), ny * nz)
    top = jnp.max(every[:, 0], axis=0)
    total = jnp.sum(every[:, 1] * jnp.exp(every[:, 0] - top), axis=0)
    lse = spread(top + jnp.log(total), "core", 2).reshape(rows)
    mass = jnp.sum(jnp.exp(scores - lse[:, None]), axis=0)
    summed = jnp.sum(spread(mass, "kvh", lax.axis_size("kvh")), axis=0)
    return summed * (total_len / LAST / HEADS)


def attend_kernel(ids, bias, q, kv, out, k_vert, v_vert, k_near, v_near, s_buf, sems):
    near = NS
    copies = []
    n = 0

    def fetch(block, which, target):
        nonlocal n
        row = pl.multiple_of((block % 2) * BLK, BLK)
        copies.append(pltpu.make_async_copy(kv.at[block // 2, which, pl.ds(row, BLK)], target, sems.at[n]))
        copies[-1].start()
        n += 1

    for j in range(NV):
        fetch(ids[0, near + j], 0, k_vert.at[pl.ds(j * BLK, BLK)])
        fetch(ids[0, near + j], 1, v_vert.at[pl.ds(j * BLK, BLK)])
    for e in range(2):
        for j in range(near):
            fetch(ids[e, j], 0, k_near.at[e, pl.ds(j * BLK, BLK)])
            fetch(ids[e, j], 1, v_near.at[e, pl.ds(j * BLK, BLK)])
    for copy in copies:
        copy.wait()

    factor = LOG2E / math.sqrt(HD)
    nt = (((1,), (1,)), ((), ()))
    width_near = near * BLK
    causal = lax.broadcasted_iota(jnp.int32, (BLK, BLK), 1) <= lax.broadcasted_iota(jnp.int32, (BLK, BLK), 0)

    def scores(i):
        e, h = i % 2, i // 2
        tile = q[h, pl.ds(pl.multiple_of(e * BLK, BLK), BLK), :]
        a = lax.dot_general(tile, k_near[e], nt, preferred_element_type=jnp.float32) * factor + bias[e, :, :width_near]
        a = jnp.concatenate([jnp.where(causal, a[:, :BLK], FAR), a[:, BLK:]], axis=1)
        b = lax.dot_general(tile, k_vert[...], nt, preferred_element_type=jnp.float32) * factor + bias[e, :, width_near:]
        s_buf[i % 2, :, :width_near] = a
        s_buf[i % 2, :, width_near:] = b
        return jnp.maximum(jnp.max(a, axis=1, keepdims=True), jnp.max(b, axis=1, keepdims=True))

    def finish(i, top):
        e, h = i % 2, i // 2
        p = jnp.exp2(s_buf[i % 2] - top)
        total = jnp.sum(p, axis=1, keepdims=True)
        w = p.astype(jnp.bfloat16)
        o = jnp.dot(w[:, :width_near], v_near[e], preferred_element_type=jnp.float32)
        o += jnp.dot(w[:, width_near:], v_vert[...], preferred_element_type=jnp.float32)
        out[h, pl.ds(pl.multiple_of(e * BLK, BLK), BLK), :] = (o / total).astype(jnp.bfloat16)

    def step(i, top):
        later = scores(i + 1)
        finish(i, top)
        return later

    tiles = 2 * GROUP
    top = lax.fori_loop(0, tiles - 1, step, scores(0))
    finish(tiles - 1, top)


def attend(ids, bias, q_t, kv):
    local = q_t.shape[1]
    vmem = pl.BlockSpec(memory_space=pltpu.VMEM)
    return pl.pallas_call(
        attend_kernel,
        out_shape=jax.ShapeDtypeStruct((GROUP, local, HD), jnp.bfloat16),
        in_specs=[pl.BlockSpec(memory_space=pltpu.SMEM), vmem, vmem, pl.BlockSpec(memory_space=pl.ANY)],
        out_specs=vmem,
        scratch_shapes=[
            pltpu.VMEM((NV * BLK, HD), jnp.bfloat16),
            pltpu.VMEM((NV * BLK, HD), jnp.bfloat16),
            pltpu.VMEM((2, NS * BLK, HD), jnp.bfloat16),
            pltpu.VMEM((2, NS * BLK, HD), jnp.bfloat16),
            pltpu.VMEM((2, BLK, (NV + NS) * BLK), jnp.float32),
            pltpu.SemaphoreType.DMA((2 * NV + 4 * NS,)),
        ],
        compiler_params=pltpu.CompilerParams(vmem_limit_bytes=56 * 1024 * 1024),
        cost_estimate=pl.CostEstimate(flops=4 * 2 * GROUP * (NV + NS) * BLK**3, bytes_accessed=4 * 1024 * 1024, transcendentals=2 * GROUP * (NV + NS) * BLK**2),
    )(ids, bias, q_t, kv)


def lists(vertical, slash_offsets, position):
    own = (position * 2 + jnp.arange(2, dtype=jnp.int32))[:, None]
    slash = slash_offsets[0]
    others = jnp.where(slash[1:] == 0, slash[0], slash[1:])
    near = own - jnp.concatenate([jnp.zeros((1,), jnp.int32), others])[None, :]
    far = jnp.broadcast_to(vertical[0][None, :], (2, NV))
    again = jnp.any(far[:, :, None] == near[:, None, :], axis=-1)
    usable = jnp.concatenate([near >= 0, (far <= own) & jnp.logical_not(again)], axis=1)
    ids = jnp.maximum(jnp.concatenate([near, far], axis=1), 0)
    bias = jnp.where(usable, 0.0, FAR).astype(jnp.float32)
    bias = jnp.broadcast_to(bias[:, None, :, None], (2, 1, NV + NS, BLK)).reshape(2, 1, (NV + NS) * BLK)
    return ids, bias


def solution(mesh):
    ny, nz = 8, 4
    wide = Mesh(mesh.devices.reshape(ny, nz, 2, -1), ("y", "zh", "core", "kvh"))

    def on_device(queries, key_rows, value_rows, vertical, slash_offsets):
        local = key_rows.shape[0]
        position = (lax.axis_index("y") * nz + lax.axis_index("zh")) * 2 + lax.axis_index("core")
        q_t = jnp.transpose(queries, (1, 0, 2))
        k, v = key_rows[:, 0], value_rows[:, 0]
        kv = lax.all_gather(jnp.stack([k, v]), CTX)
        profile = estimate(q_t, k, position, local, ny, nz)
        ids, bias = lists(vertical, slash_offsets, position)
        attended = attend(ids, bias, q_t, kv)
        return jnp.transpose(attended, (1, 0, 2)), profile

    return jax.shard_map(
        on_device,
        mesh=wide,
        in_specs=(P(CTX, "kvh", None), P(CTX, "kvh", None), P(CTX, "kvh", None), P("kvh", None), P("kvh", None)),
        out_specs=(P(CTX, "kvh", None), P(CTX)),
        check_vma=False,
    )
```

```python
import functools
import math

import jax
import jax.numpy as jnp
from jax import lax
from jax.experimental import pallas as pl
from jax.experimental.pallas import tpu as pltpu
from jax.sharding import Mesh
from jax.sharding import PartitionSpec as P

BLK = 128
LAST = 64
NV = 16
NS = 8
HEADS = 40
HD = 128
GROUP = 5
FAR = -1e30
LOG2E = math.log2(math.e)
C = ("zh", "core")
CTX = ("y", "zh", "core")
NY, NZ = 8, 4
PER_ROW = 2 * NZ
PIECE = BLK // NY
LISTED = NV * PIECE
QROWS = 48
QALL = NY * QROWS
QREAL = GROUP * LAST
NT = (((1,), (1,)), ((), ()))
SMEM = pl.BlockSpec(memory_space=pltpu.SMEM)
VMEM = pl.BlockSpec(memory_space=pltpu.VMEM)
ANY = pl.BlockSpec(memory_space=pl.ANY)
F32 = jnp.float32
BF16 = jnp.bfloat16
LARGE = pltpu.CompilerParams(vmem_limit_bytes=60 * 1024 * 1024)
SMALL = pltpu.CompilerParams(vmem_limit_bytes=8 * 1024 * 1024)


def shape(kind, *dims):
    return jax.ShapeDtypeStruct(dims, kind)


def exchange(x, axis):
    return lax.all_to_all(x, axis, 0, 0)


def pack_kernel(q, k, v, sent, kv, last, sem):
    local = k.shape[0]
    copy = pltpu.make_async_copy(q.at[:, pl.ds(local - LAST, LAST)], last, sem)
    copy.start()
    for which, x in enumerate((k, v)):
        kv[which] = x[...]
        for y in range(NY):
            for b in range(2):
                sent[2 * y + which, b * PIECE : (b + 1) * PIECE, :] = x[b * BLK + y * PIECE : b * BLK + (y + 1) * PIECE, :]
    copy.wait()
    flat = last[...].reshape(QREAL, HD)
    flat = jnp.concatenate([flat, jnp.zeros((QALL - QREAL, HD), BF16)], axis=0)
    for d in range(2 * NY):
        sent[d, 2 * PIECE :, :] = flat[d // 2 * QROWS : (d // 2 + 1) * QROWS]


def pack(q_t, k, v):
    return pl.pallas_call(
        pack_kernel,
        out_shape=(shape(BF16, 2 * NY, 2 * PIECE + QROWS, HD), shape(BF16, 2, *k.shape)),
        in_specs=[ANY, VMEM, VMEM],
        out_specs=(VMEM, VMEM),
        scratch_shapes=[pltpu.VMEM((GROUP, LAST, HD), BF16), pltpu.SemaphoreType.DMA],
        compiler_params=LARGE,
    )(q_t, k, v)


def pick_kernel(ids, zh, r, after, out):
    for j in range(NV):
        c = ids[0, j]
        source = (c // 16) * 2 + (c // 2) % 2
        tile = r[source, pl.ds(pl.multiple_of((c % 2) * PIECE, PIECE), PIECE), :]
        tile = jnp.where((c // 4) % NZ == zh[0], tile, jnp.zeros_like(tile))
        for d in range(NZ):
            out[d, j * PIECE : (j + 1) * PIECE, :] = tile
    for d in range(NZ):
        out[d, LISTED:, :] = r[2 * NY - 1, 2 * PIECE :, :]


def pick(vertical, zh, r, after):
    return pl.pallas_call(
        pick_kernel,
        out_shape=shape(BF16, NZ, LISTED + QROWS, HD),
        in_specs=[SMEM, SMEM, VMEM, ANY],
        out_specs=VMEM,
        compiler_params=SMALL,
    )(vertical, zh, r, after)


def merge_kernel(r, out):
    whole = r[0, :LISTED, :]
    for z in range(1, NZ):
        whole = whole + r[z, :LISTED, :]
    for d in range(NY):
        out[d, :LISTED, :] = whole
        out[d, LISTED:, :] = r[NZ - 1, LISTED:, :]


def merge(r):
    return pl.pallas_call(merge_kernel, out_shape=shape(BF16, NY, LISTED + QROWS, HD), in_specs=[VMEM], out_specs=VMEM, compiler_params=SMALL)(r)


def estimate_kernel(total_len, position, r, k, scores, stats):
    local = k.shape[0]
    q = r[:, LISTED:, :].reshape(QALL, HD)
    s = lax.dot_general(k[...], q, NT, preferred_element_type=F32) * (1.0 / math.sqrt(HD))
    key_pos = position[0] * local + lax.broadcasted_iota(jnp.int32, (local, QALL), 0)
    last_pos = total_len - LAST + lax.broadcasted_iota(jnp.int32, (local, QALL), 1) % LAST
    s = jnp.where(key_pos <= last_pos, s, FAR)
    scores[...] = s
    top = jnp.max(s, axis=0, keepdims=True)
    total = jnp.sum(jnp.exp(s - top), axis=0, keepdims=True)
    both = jnp.concatenate([top, total], axis=0)
    for d in range(2 * NY):
        stats[d] = both


def estimate(position, r, k, total_len):
    local = k.shape[0]
    return pl.pallas_call(
        functools.partial(estimate_kernel, total_len),
        out_shape=(shape(F32, local, QALL), shape(F32, 2 * NY, 2, QALL)),
        in_specs=[SMEM, VMEM, VMEM],
        out_specs=(VMEM, VMEM),
        compiler_params=SMALL,
    )(position, r, k)


def joined(stats):
    n = stats.shape[0]
    top = stats[0, 0:1, :]
    for i in range(1, n):
        top = jnp.maximum(top, stats[i, 0:1, :])
    total = jnp.zeros_like(top)
    for i in range(n):
        total += stats[i, 1:2, :] * jnp.exp(stats[i, 0:1, :] - top)
    return top, total


def join_kernel(stats, after, out):
    both = jnp.concatenate(joined(stats), axis=0)
    for d in range(NZ):
        out[d] = both


def join(stats, after):
    return pl.pallas_call(join_kernel, out_shape=shape(F32, NZ, 2, QALL), in_specs=[VMEM, ANY], out_specs=VMEM, compiler_params=SMALL)(stats, after)


def mass_kernel(stats, scores, after, out):
    top, total = joined(stats)
    p = jnp.exp(scores[...] - (top + jnp.log(total)))
    real = (lax.broadcasted_iota(jnp.int32, (out.shape[0], QALL), 1) < QREAL).astype(F32)
    out[:, 0, :] = lax.dot_general(real, p, NT, precision=lax.Precision.HIGHEST, preferred_element_type=F32)


def mass(stats, scores, after, kvh):
    return pl.pallas_call(
        mass_kernel,
        out_shape=shape(F32, kvh, 1, scores.shape[0]),
        in_specs=[VMEM, VMEM, ANY],
        out_specs=VMEM,
        compiler_params=SMALL,
    )(stats, scores, after)


def attend_kernel(first, count, places, core, bias, q, mine, theirs, rows, earlier, *rest):
    if first:
        rest = rest[1:]
    out, token, q_buf, k_vert, v_vert, k_near, v_near, s_buf, o_buf, sems = rest
    token[...] = jnp.zeros_like(token)
    copies = []
    sem = lambda: sems.at[len(copies)]

    copies.append(pltpu.make_async_copy(q.at[pl.ds(first, count)], q_buf, sem()))
    copies[-1].start()
    for e in range(2):
        for j in range(NS):
            place = places[e, j]
            row = pl.ds(pl.multiple_of((place % 2) * BLK, BLK), BLK)
            for which, target in ((0, k_near), (1, v_near)):
                target = target.at[e, pl.ds(j * BLK, BLK)]
                copy = pltpu.make_async_copy(rows.at[place // 4, which, row], target, sem())
                other = pltpu.make_async_copy(earlier.at[place // 4, which, row], target, sem())
                pl.when((place // 2) % 2 == 0)(copy.start)
                pl.when((place // 2) % 2 == 1)(other.start)
                copies.append(copy)
    for which, target in ((0, k_vert), (1, v_vert)):
        copy = pltpu.make_async_copy(mine.at[:, pl.ds(0, LISTED)], target, sem())
        other = pltpu.make_async_copy(theirs.at[:, pl.ds(0, LISTED)], target, sem())
        pl.when(core[0] == which)(copy.start)
        pl.when(core[0] != which)(other.start)
        copies.append(copy)
    for copy in copies:
        copy.wait()

    factor = LOG2E / math.sqrt(HD)
    width_near = NS * BLK
    causal = lax.broadcasted_iota(jnp.int32, (BLK, BLK), 1) <= lax.broadcasted_iota(jnp.int32, (BLK, BLK), 0)

    def scores(i):
        e, h = i % 2, i // 2
        tile = q_buf[h, pl.ds(pl.multiple_of(e * BLK, BLK), BLK), :]
        a = lax.dot_general(tile, k_near[e], NT, preferred_element_type=F32) * factor + bias[e, :, :width_near]
        a = jnp.concatenate([jnp.where(causal, a[:, :BLK], FAR), a[:, BLK:]], axis=1)
        keys = k_vert[...].reshape(NV * BLK, HD)
        b = lax.dot_general(tile, keys, NT, preferred_element_type=F32) * factor + bias[e, :, width_near:]
        s_buf[i % 2, :, :width_near] = a
        s_buf[i % 2, :, width_near:] = b
        return jnp.maximum(jnp.max(a, axis=1, keepdims=True), jnp.max(b, axis=1, keepdims=True))

    def finish(i, top):
        e, h = i % 2, i // 2
        p = jnp.exp2(s_buf[i % 2] - top)
        total = jnp.sum(p, axis=1, keepdims=True)
        w = p.astype(BF16)
        o = jnp.dot(w[:, :width_near], v_near[e], preferred_element_type=F32)
        o += jnp.dot(w[:, width_near:], v_vert[...].reshape(NV * BLK, HD), preferred_element_type=F32)
        o_buf[h, pl.ds(pl.multiple_of(e * BLK, BLK), BLK), :] = (o / total).astype(BF16)

    def step(i, top):
        later = scores(i + 1)
        finish(i, top)
        return later

    tiles = 2 * count
    top = lax.fori_loop(0, tiles - 1, step, scores(0))
    finish(tiles - 1, top)
    copy = pltpu.make_async_copy(o_buf, out.at[pl.ds(first, count)], sems.at[0])
    copy.start()
    copy.wait()


def attend(first, count, places, core, bias, q_t, mine, theirs, rows, earlier, out=None):
    local = q_t.shape[1]
    args = (places, core, bias, q_t, mine, theirs, rows, earlier) + ((out,) if first else ())
    return pl.pallas_call(
        functools.partial(attend_kernel, first, count),
        out_shape=(shape(BF16, GROUP, local, HD), shape(F32, 8, 128)),
        in_specs=[SMEM, SMEM, VMEM] + [ANY] * (len(args) - 3),
        out_specs=(ANY, VMEM),
        scratch_shapes=[
            pltpu.VMEM((count, local, HD), BF16),
            pltpu.VMEM((NY, LISTED, HD), BF16),
            pltpu.VMEM((NY, LISTED, HD), BF16),
            pltpu.VMEM((2, NS * BLK, HD), BF16),
            pltpu.VMEM((2, NS * BLK, HD), BF16),
            pltpu.VMEM((2, BLK, (NV + NS) * BLK), F32),
            pltpu.VMEM((count, local, HD), BF16),
            pltpu.SemaphoreType.DMA((4 * NS + 3,)),
        ],
        input_output_aliases={len(args) - 1: 0} if first else {},
        compiler_params=LARGE,
        cost_estimate=pl.CostEstimate(
            flops=4 * 2 * count * (NV + NS) * BLK**3, bytes_accessed=4 * 1024 * 1024, transcendentals=2 * count * (NV + NS) * BLK**2
        ),
    )(*args)


def lists(vertical, slash_offsets, position):
    own = (position * 2 + jnp.arange(2, dtype=jnp.int32))[:, None]
    slash = slash_offsets[0]
    others = jnp.where(slash[1:] == 0, slash[0], slash[1:])
    near = own - jnp.concatenate([jnp.zeros((1,), jnp.int32), others])[None, :]
    far = jnp.broadcast_to(vertical[0][None, :], (2, NV))
    again = jnp.any(far[:, :, None] == near[:, None, :], axis=-1)
    usable = jnp.concatenate([near >= 0, (far <= own) & jnp.logical_not(again)], axis=1)
    bias = jnp.where(usable, 0.0, FAR).astype(F32)
    by_near = jnp.broadcast_to(bias[:, None, :NS, None], (2, 1, NS, BLK)).reshape(2, 1, NS * BLK)
    by_far = jnp.broadcast_to(bias[:, None, None, NS:, None], (2, 1, NY, NV, PIECE)).reshape(2, 1, NV * BLK)
    bias = jnp.concatenate([by_near, by_far], axis=2)
    kept = jnp.maximum(near, 0)
    before = (kept // 2 // PER_ROW != position // PER_ROW).astype(jnp.int32)
    places = ((kept // 2) % PER_ROW * 2 + before) * 2 + kept % 2
    return places, bias


def on_device(queries, key_rows, value_rows, vertical, slash_offsets):
    local = key_rows.shape[0]
    total_len = local * NY * PER_ROW
    zh, core = lax.axis_index("zh"), lax.axis_index("core")
    position = (lax.axis_index("y") * NZ + zh) * 2 + core
    q_t = jnp.transpose(queries, (1, 0, 2))
    k, v = key_rows[:, 0], value_rows[:, 0]

    sent, kv = pack(q_t, k, v)
    before = lax.ppermute(kv, "y", [(i, (i + 1) % NY) for i in range(NY)])
    rows, earlier = lax.all_gather(kv, C), lax.all_gather(before, C)
    r = exchange(sent, ("y", "core"))
    r = exchange(pick(vertical, zh.reshape(1), r, before), "zh")
    mine = exchange(merge(r), "y")
    theirs = lax.ppermute(mine, "core", [(0, 1), (1, 0)])
    scores, stats = estimate(position.reshape(1), mine, k, total_len)

    places, bias = lists(vertical, slash_offsets, position)
    given = (places, core.reshape(1), bias, q_t, mine, theirs, rows, earlier)
    out, token = attend(0, 2, *given)
    stats = exchange(join(exchange(stats, ("y", "core")), token), "zh")
    out, token = attend(2, 2, *given, out)
    part = exchange(mass(stats, scores, token, lax.axis_size("kvh")), "kvh")
    out, token = attend(4, 1, *given, out)
    profile = jnp.sum(part, axis=(0, 1)) * (total_len / LAST / HEADS)
    return jnp.transpose(out, (1, 0, 2)), profile


def solution(mesh):
    wide = Mesh(mesh.devices.reshape(NY, NZ, 2, -1), ("y", "zh", "core", "kvh"))
    return jax.shard_map(
        on_device,
        mesh=wide,
        in_specs=(P(CTX, "kvh", None), P(CTX, "kvh", None), P(CTX, "kvh", None), P("kvh", None), P("kvh", None)),
        out_specs=(P(CTX, "kvh", None), P(CTX)),
        check_vma=False,
    )
```

```python
import functools
import math

import jax
import jax.numpy as jnp
from jax import lax
from jax.experimental import pallas as pl
from jax.experimental.pallas import tpu as pltpu
from jax.sharding import Mesh
from jax.sharding import PartitionSpec as P

BLK = 128
LAST = 64
NV = 16
NS = 8
HEADS = 40
HD = 128
GROUP = 5
FAR = -1e30
LOG2E = math.log2(math.e)
C = ("zh", "core")
CTX = ("y", "zh", "core")
NY, NZ = 8, 4
PER_ROW = 2 * NZ
PIECE = BLK // NY
LISTED = NV * PIECE
QROWS = 48
QALL = NY * QROWS
QREAL = GROUP * LAST
NT = (((1,), (1,)), ((), ()))
SMEM = pl.BlockSpec(memory_space=pltpu.SMEM)
VMEM = pl.BlockSpec(memory_space=pltpu.VMEM)
ANY = pl.BlockSpec(memory_space=pl.ANY)
F32 = jnp.float32
BF16 = jnp.bfloat16
LARGE = pltpu.CompilerParams(vmem_limit_bytes=60 * 1024 * 1024)
SMALL = pltpu.CompilerParams(vmem_limit_bytes=8 * 1024 * 1024)


def shape(kind, *dims):
    return jax.ShapeDtypeStruct(dims, kind)


def exchange(x, axis):
    return lax.all_to_all(x, axis, 0, 0)


def pack_kernel(q, k, v, sent, kv, last, sem):
    local = k.shape[0]
    copy = pltpu.make_async_copy(q.at[:, pl.ds(local - LAST, LAST)], last, sem)
    copy.start()
    for which, x in enumerate((k, v)):
        kv[which] = x[...]
        for y in range(NY):
            for b in range(2):
                sent[2 * y + which, b * PIECE : (b + 1) * PIECE, :] = x[b * BLK + y * PIECE : b * BLK + (y + 1) * PIECE, :]
    copy.wait()
    flat = last[...].reshape(QREAL, HD)
    flat = jnp.concatenate([flat, jnp.zeros((QALL - QREAL, HD), BF16)], axis=0)
    for d in range(2 * NY):
        sent[d, 2 * PIECE :, :] = flat[d // 2 * QROWS : (d // 2 + 1) * QROWS]


def pack(q_t, k, v):
    return pl.pallas_call(
        pack_kernel,
        out_shape=(shape(BF16, 2 * NY, 2 * PIECE + QROWS, HD), shape(BF16, 2, *k.shape)),
        in_specs=[ANY, VMEM, VMEM],
        out_specs=(VMEM, VMEM),
        scratch_shapes=[pltpu.VMEM((GROUP, LAST, HD), BF16), pltpu.SemaphoreType.DMA],
        compiler_params=LARGE,
    )(q_t, k, v)


def pick_kernel(ids, zh, r, out):
    for j in range(NV):
        c = ids[0, j]
        source = (c // 16) * 2 + (c // 2) % 2
        tile = r[source, pl.ds(pl.multiple_of((c % 2) * PIECE, PIECE), PIECE), :]
        tile = jnp.where((c // 4) % NZ == zh[0], tile, jnp.zeros_like(tile))
        for d in range(NZ):
            out[d, j * PIECE : (j + 1) * PIECE, :] = tile
    for d in range(NZ):
        out[d, LISTED:, :] = r[2 * NY - 1, 2 * PIECE :, :]


def pick(vertical, zh, r):
    return pl.pallas_call(
        pick_kernel,
        out_shape=shape(BF16, NZ, LISTED + QROWS, HD),
        in_specs=[SMEM, SMEM, VMEM],
        out_specs=VMEM,
        compiler_params=SMALL,
    )(vertical, zh, r)


def merge_kernel(r, kv, after, out, again):
    again[...] = kv[...]
    whole = r[0, :LISTED, :]
    for z in range(1, NZ):
        whole = whole + r[z, :LISTED, :]
    for d in range(NY):
        out[d, :LISTED, :] = whole
        out[d, LISTED:, :] = r[NZ - 1, LISTED:, :]


def merge(r, kv, after):
    return pl.pallas_call(
        merge_kernel,
        out_shape=(shape(BF16, NY, LISTED + QROWS, HD), shape(BF16, *kv.shape)),
        in_specs=[VMEM, VMEM, ANY],
        out_specs=(VMEM, VMEM),
        compiler_params=SMALL,
    )(r, kv, after)


def together_kernel(*refs):
    *parts, out, sems = refs
    copies = [pltpu.make_async_copy(part, out.at[i], sems.at[i]) for i, part in enumerate(parts)]
    for copy in copies:
        copy.start()
    for copy in copies:
        copy.wait()


def together(parts):
    return pl.pallas_call(
        together_kernel,
        out_shape=shape(BF16, len(parts), *parts[0].shape),
        in_specs=[ANY] * len(parts),
        out_specs=ANY,
        scratch_shapes=[pltpu.SemaphoreType.DMA((len(parts),))],
        compiler_params=SMALL,
    )(*parts)


def estimate_kernel(total_len, position, r, k, scores, stats):
    local = k.shape[0]
    q = r[:, LISTED:, :].reshape(QALL, HD)
    s = lax.dot_general(k[...], q, NT, preferred_element_type=F32) * (1.0 / math.sqrt(HD))
    key_pos = position[0] * local + lax.broadcasted_iota(jnp.int32, (local, QALL), 0)
    last_pos = total_len - LAST + lax.broadcasted_iota(jnp.int32, (local, QALL), 1) % LAST
    s = jnp.where(key_pos <= last_pos, s, FAR)
    scores[...] = s
    top = jnp.max(s, axis=0, keepdims=True)
    total = jnp.sum(jnp.exp(s - top), axis=0, keepdims=True)
    both = jnp.concatenate([top, total], axis=0)
    for d in range(2 * NY):
        stats[d] = both


def estimate(position, r, k, total_len):
    local = k.shape[0]
    return pl.pallas_call(
        functools.partial(estimate_kernel, total_len),
        out_shape=(shape(F32, local, QALL), shape(F32, 2 * NY, 2, QALL)),
        in_specs=[SMEM, VMEM, VMEM],
        out_specs=(VMEM, VMEM),
        compiler_params=SMALL,
    )(position, r, k)


def joined(stats):
    n = stats.shape[0]
    top = stats[0, 0:1, :]
    for i in range(1, n):
        top = jnp.maximum(top, stats[i, 0:1, :])
    total = jnp.zeros_like(top)
    for i in range(n):
        total += stats[i, 1:2, :] * jnp.exp(stats[i, 0:1, :] - top)
    return top, total


def join_kernel(stats, after, out):
    both = jnp.concatenate(joined(stats), axis=0)
    for d in range(NZ):
        out[d] = both


def join(stats, after):
    return pl.pallas_call(join_kernel, out_shape=shape(F32, NZ, 2, QALL), in_specs=[VMEM, ANY], out_specs=VMEM, compiler_params=SMALL)(stats, after)


def mass_kernel(stats, scores, after, out):
    top, total = joined(stats)
    p = jnp.exp(scores[...] - (top + jnp.log(total)))
    real = (lax.broadcasted_iota(jnp.int32, (out.shape[0], QALL), 1) < QREAL).astype(F32)
    out[:, 0, :] = lax.dot_general(real, p, NT, precision=lax.Precision.HIGHEST, preferred_element_type=F32)


def mass(stats, scores, after, kvh):
    return pl.pallas_call(
        mass_kernel,
        out_shape=shape(F32, kvh, 1, scores.shape[0]),
        in_specs=[VMEM, VMEM, ANY],
        out_specs=VMEM,
        compiler_params=SMALL,
    )(stats, scores, after)


def attend_kernel(first, count, places, core, bias, q, mine, theirs, near, near_theirs, *rest):
    if first:
        rest = rest[1:]
    out, token, q_buf, k_vert, v_vert, k_near, v_near, s_buf, o_buf, sems = rest
    token[...] = jnp.zeros_like(token)
    copies = []
    sem = lambda: sems.at[len(copies)]

    copies.append(pltpu.make_async_copy(q.at[pl.ds(first, count)], q_buf, sem()))
    copies[-1].start()
    for e in range(2):
        for j in range(NS):
            place = places[e, j]
            row = pl.ds(pl.multiple_of((place % 2) * BLK, BLK), BLK)
            for which, target in ((0, k_near), (1, v_near)):
                target = target.at[e, pl.ds(j * BLK, BLK)]
                copy = pltpu.make_async_copy(near.at[place // 4, which, row], target, sem())
                other = pltpu.make_async_copy(near_theirs.at[place // 4, which, row], target, sem())
                pl.when((place // 2) % 2 == core[0])(copy.start)
                pl.when((place // 2) % 2 != core[0])(other.start)
                copies.append(copy)
    for which, target in ((0, k_vert), (1, v_vert)):
        copy = pltpu.make_async_copy(mine.at[:, pl.ds(0, LISTED)], target, sem())
        other = pltpu.make_async_copy(theirs.at[:, pl.ds(0, LISTED)], target, sem())
        pl.when(core[0] == which)(copy.start)
        pl.when(core[0] != which)(other.start)
        copies.append(copy)
    for copy in copies:
        copy.wait()

    factor = LOG2E / math.sqrt(HD)
    width_near = NS * BLK
    causal = lax.broadcasted_iota(jnp.int32, (BLK, BLK), 1) <= lax.broadcasted_iota(jnp.int32, (BLK, BLK), 0)

    def scores(i):
        e, h = i % 2, i // 2
        tile = q_buf[h, pl.ds(pl.multiple_of(e * BLK, BLK), BLK), :]
        a = lax.dot_general(tile, k_near[e], NT, preferred_element_type=F32) * factor + bias[e, :, :width_near]
        a = jnp.concatenate([jnp.where(causal, a[:, :BLK], FAR), a[:, BLK:]], axis=1)
        keys = k_vert[...].reshape(NV * BLK, HD)
        b = lax.dot_general(tile, keys, NT, preferred_element_type=F32) * factor + bias[e, :, width_near:]
        s_buf[i % 2, :, :width_near] = a
        s_buf[i % 2, :, width_near:] = b
        return jnp.maximum(jnp.max(a, axis=1, keepdims=True), jnp.max(b, axis=1, keepdims=True))

    def finish(i, top):
        e, h = i % 2, i // 2
        p = jnp.exp2(s_buf[i % 2] - top)
        total = jnp.sum(p, axis=1, keepdims=True)
        w = p.astype(BF16)
        o = jnp.dot(w[:, :width_near], v_near[e], preferred_element_type=F32)
        o += jnp.dot(w[:, width_near:], v_vert[...].reshape(NV * BLK, HD), preferred_element_type=F32)
        o_buf[h, pl.ds(pl.multiple_of(e * BLK, BLK), BLK), :] = (o / total).astype(BF16)

    def step(i, top):
        later = scores(i + 1)
        finish(i, top)
        return later

    tiles = 2 * count
    top = lax.fori_loop(0, tiles - 1, step, scores(0))
    finish(tiles - 1, top)
    copy = pltpu.make_async_copy(o_buf, out.at[pl.ds(first, count)], sems.at[0])
    copy.start()
    copy.wait()


def attend(first, count, places, core, bias, q_t, mine, theirs, near, near_theirs, out=None):
    local = q_t.shape[1]
    args = (places, core, bias, q_t, mine, theirs, near, near_theirs) + ((out,) if first else ())
    return pl.pallas_call(
        functools.partial(attend_kernel, first, count),
        out_shape=(shape(BF16, GROUP, local, HD), shape(F32, 8, 128)),
        in_specs=[SMEM, SMEM, VMEM] + [ANY] * (len(args) - 3),
        out_specs=(ANY, VMEM),
        scratch_shapes=[
            pltpu.VMEM((count, local, HD), BF16),
            pltpu.VMEM((NY, LISTED, HD), BF16),
            pltpu.VMEM((NY, LISTED, HD), BF16),
            pltpu.VMEM((2, NS * BLK, HD), BF16),
            pltpu.VMEM((2, NS * BLK, HD), BF16),
            pltpu.VMEM((2, BLK, (NV + NS) * BLK), F32),
            pltpu.VMEM((count, local, HD), BF16),
            pltpu.SemaphoreType.DMA((4 * NS + 3,)),
        ],
        input_output_aliases={len(args) - 1: 0} if first else {},
        compiler_params=LARGE,
        cost_estimate=pl.CostEstimate(
            flops=4 * 2 * count * (NV + NS) * BLK**3, bytes_accessed=4 * 1024 * 1024, transcendentals=2 * count * (NV + NS) * BLK**2
        ),
    )(*args)


def lists(vertical, slash_offsets, position):
    own = (position * 2 + jnp.arange(2, dtype=jnp.int32))[:, None]
    slash = slash_offsets[0]
    others = jnp.where(slash[1:] == 0, slash[0], slash[1:])
    near = own - jnp.concatenate([jnp.zeros((1,), jnp.int32), others])[None, :]
    far = jnp.broadcast_to(vertical[0][None, :], (2, NV))
    again = jnp.any(far[:, :, None] == near[:, None, :], axis=-1)
    usable = jnp.concatenate([near >= 0, (far <= own) & jnp.logical_not(again)], axis=1)
    bias = jnp.where(usable, 0.0, FAR).astype(F32)
    by_near = jnp.broadcast_to(bias[:, None, :NS, None], (2, 1, NS, BLK)).reshape(2, 1, NS * BLK)
    by_far = jnp.broadcast_to(bias[:, None, None, NS:, None], (2, 1, NY, NV, PIECE)).reshape(2, 1, NV * BLK)
    bias = jnp.concatenate([by_near, by_far], axis=2)
    kept = jnp.where(near >= 0, near, own)
    places = (position // 2 - kept // 4) * 4 + kept % 4
    return places, bias


def on_device(queries, key_rows, value_rows, vertical, slash_offsets):
    local = key_rows.shape[0]
    total_len = local * NY * PER_ROW
    zh, core = lax.axis_index("zh"), lax.axis_index("core")
    position = (lax.axis_index("y") * NZ + zh) * 2 + core
    q_t = jnp.transpose(queries, (1, 0, 2))
    k, v = key_rows[:, 0], value_rows[:, 0]

    sent, kv = pack(q_t, k, v)
    back = lambda x, chips: lax.ppermute(x, ("y", "zh"), [(i, (i + chips) % (NY * NZ)) for i in range(NY * NZ)])
    other_core = [(0, 1), (1, 0)]
    four = back(kv, 4)
    r = exchange(sent, ("y", "core"))
    r = exchange(pick(vertical, zh.reshape(1), r), "zh")
    whole, kv = merge(r, kv, four)
    mine = exchange(whole, "y")
    near = together([kv, back(kv, 1), back(kv, 2), back(kv, 3), four])
    near_theirs = lax.ppermute(near, "core", other_core)
    theirs = lax.ppermute(mine, "core", other_core)
    scores, stats = estimate(position.reshape(1), mine, k, total_len)

    places, bias = lists(vertical, slash_offsets, position)
    given = (places, core.reshape(1), bias, q_t, mine, theirs, near, near_theirs)
    out, token = attend(0, 2, *given)
    stats = exchange(join(exchange(stats, ("y", "core")), token), "zh")
    out, token = attend(2, 2, *given, out)
    part = exchange(mass(stats, scores, token, lax.axis_size("kvh")), "kvh")
    out, token = attend(4, 1, *given, out)
    profile = jnp.sum(part, axis=(0, 1)) * (total_len / LAST / HEADS)
    return jnp.transpose(out, (1, 0, 2)), profile


def solution(mesh):
    wide = Mesh(mesh.devices.reshape(NY, NZ, 2, -1), ("y", "zh", "core", "kvh"))
    return jax.shard_map(
        on_device,
        mesh=wide,
        in_specs=(P(CTX, "kvh", None), P(CTX, "kvh", None), P(CTX, "kvh", None), P("kvh", None), P("kvh", None)),
        out_specs=(P(CTX, "kvh", None), P(CTX)),
        check_vma=False,
    )
```

```python
import functools
import math

import jax
import jax.numpy as jnp
from jax import lax
from jax.experimental import pallas as pl
from jax.experimental.pallas import tpu as pltpu
from jax.sharding import Mesh
from jax.sharding import PartitionSpec as P

BLK = 128
LAST = 64
NV = 16
NS = 8
HEADS = 40
HD = 128
GROUP = 5
FAR = -1e30
LOG2E = math.log2(math.e)
C = ("zh", "core")
CTX = ("y", "zh", "core")
NY, NZ = 8, 4
PER_ROW = 2 * NZ
CHIPS = NY * NZ
PIECE = BLK // CHIPS
LISTED = NV * PIECE
UNIT = NZ * LISTED
NEAR = NS * BLK // UNIT
BACK = 5
QROWS = 16
QREAL = GROUP * LAST // 2
QALL = 256
NT = (((1,), (1,)), ((), ()))
SMEM = pl.BlockSpec(memory_space=pltpu.SMEM)
VMEM = pl.BlockSpec(memory_space=pltpu.VMEM)
ANY = pl.BlockSpec(memory_space=pl.ANY)
F32 = jnp.float32
BF16 = jnp.bfloat16
LARGE = pltpu.CompilerParams(vmem_limit_bytes=60 * 1024 * 1024)
SMALL = pltpu.CompilerParams(vmem_limit_bytes=8 * 1024 * 1024)


def shape(kind, *dims):
    return jax.ShapeDtypeStruct(dims, kind)


def exchange(x, axis):
    return lax.all_to_all(x, axis, 0, 0)


def pack_kernel(position, q, k, v, sent, kv, last, sem):
    local = k.shape[0]
    copy = pltpu.make_async_copy(q.at[:, pl.ds(local - LAST, LAST)], last, sem)
    copy.start()
    both = jnp.concatenate([k[...], v[...]], axis=0)
    kv[...] = both.reshape(kv.shape)
    n = 2 * local
    row = lax.broadcasted_iota(jnp.int32, (n, n), 0)
    column = lax.broadcasted_iota(jnp.int32, (n, n), 1)
    source = ((row >> 3) & 1) * local + ((row >> 2) & 1) * BLK + (row >> 4) * PIECE + (row & 3)
    cut = jnp.dot((column == source).astype(BF16), both, preferred_element_type=F32).astype(BF16)
    sent[...] = cut.reshape(sent.shape)
    copy.wait()

    @pl.when(position[0] == 2 * CHIPS - 1)
    def _():
        flat = last[...].reshape(GROUP * LAST, HD)
        flat = jnp.concatenate([flat, jnp.zeros((n - GROUP * LAST, HD), BF16)], axis=0)
        sent[...] = flat.reshape(sent.shape)


def pack(position, q_t, k, v):
    local = k.shape[0]
    return pl.pallas_call(
        pack_kernel,
        out_shape=(shape(BF16, CHIPS, 16, HD), shape(BF16, 2, local, HD)),
        in_specs=[SMEM, ANY, VMEM, VMEM],
        out_specs=(VMEM, VMEM),
        scratch_shapes=[pltpu.VMEM((GROUP, LAST, HD), BF16), pltpu.SemaphoreType.DMA],
        compiler_params=LARGE,
    )(position, q_t, k, v)


def pick_kernel(ids, r, one, three, out, one_again):
    one_again[...] = one[...]
    rows = r[...].reshape(CHIPS * 16, HD)
    wanted = LISTED + QROWS
    row = lax.broadcasted_iota(jnp.int32, (wanted, HD), 0)
    source = jnp.where(row < LISTED + 8, CHIPS * 16 - 8 - LISTED + row, -1)
    for j in range(NV):
        source = jnp.where(row // PIECE == j, ids[0, j] * PIECE + row % PIECE, source)
    column = lax.broadcasted_iota(jnp.int32, (wanted, HD), 1)
    chosen = jnp.concatenate([(column + i == source).astype(BF16) for i in range(0, CHIPS * 16, HD)], axis=1)
    tile = jnp.dot(chosen, rows, preferred_element_type=F32).astype(BF16)
    for d in range(NZ):
        out[d] = tile


def pick(vertical, r, one, three):
    return pl.pallas_call(
        pick_kernel,
        out_shape=(shape(BF16, NZ, LISTED + QROWS, HD), shape(BF16, *one.shape)),
        in_specs=[SMEM, VMEM, VMEM, ANY],
        out_specs=(VMEM, VMEM),
        compiler_params=SMALL,
    )(vertical, r, one, three)


def merge_kernel(r, one, four, k_theirs, out, one_again):
    one_again[...] = one[...]
    q = jnp.concatenate([r[z, LISTED:, :].astype(F32)[:8] for z in range(NZ)], axis=0).astype(BF16)
    for d in range(NY):
        for z in range(NZ):
            out[d, z * LISTED : (z + 1) * LISTED, :] = r[z, :LISTED, :]
        out[d, UNIT:, :] = q


def merge(r, one, four, k_theirs):
    return pl.pallas_call(
        merge_kernel,
        out_shape=(shape(BF16, NY, UNIT + 8 * NZ, HD), shape(BF16, *one.shape)),
        in_specs=[VMEM, VMEM, ANY, ANY],
        out_specs=(VMEM, VMEM),
        compiler_params=SMALL,
    )(r, one, four, k_theirs)


def together_kernel(*refs):
    *parts, mine, out, sems = refs
    n = len(parts)
    each = parts[0].shape[0]
    copies = [pltpu.make_async_copy(part, out.at[pl.ds(each * i, each)], sems.at[i]) for i, part in enumerate(parts)]
    copies.append(pltpu.make_async_copy(mine.at[:, pl.ds(0, UNIT)], out.at[pl.ds(each * n, NY)], sems.at[n]))
    for copy in copies:
        copy.start()
    for copy in copies:
        copy.wait()


def together(parts, mine):
    n = len(parts)
    return pl.pallas_call(
        together_kernel,
        out_shape=shape(BF16, n * parts[0].shape[0] + NY, UNIT, HD),
        in_specs=[ANY] * (n + 1),
        out_specs=ANY,
        scratch_shapes=[pltpu.SemaphoreType.DMA((n + 1,))],
        compiler_params=SMALL,
    )(*parts, mine)


def estimate_kernel(total_len, position, r, k_mine, k_theirs, scores, stats):
    tokens = 2 * k_mine.shape[0]
    core = position[0] & 1
    q = r[:, UNIT:, :].reshape(QALL, HD)
    mine, theirs = k_mine[...], k_theirs[...]
    k = jnp.concatenate([jnp.where(core == 0, mine, theirs), jnp.where(core == 0, theirs, mine)], axis=0)
    s = lax.dot_general(k, q, NT, preferred_element_type=F32) * (1.0 / math.sqrt(HD))
    column = lax.broadcasted_iota(jnp.int32, (1, QALL), 1)
    last_pos = total_len - LAST + ((column >> 3) * 16 + core * 8 + (column & 7)) % LAST
    key_pos = (position[0] >> 1) * tokens + lax.broadcasted_iota(jnp.int32, (tokens, QALL), 0)
    s = jnp.where(key_pos <= last_pos, s, FAR)
    scores[...] = s
    top = jnp.max(s, axis=0, keepdims=True)
    total = jnp.sum(jnp.exp(s - top), axis=0, keepdims=True)
    both = jnp.concatenate([top, total], axis=0)
    for d in range(CHIPS):
        stats[d] = both


def estimate(position, r, k_mine, k_theirs, total_len):
    return pl.pallas_call(
        functools.partial(estimate_kernel, total_len),
        out_shape=(shape(F32, 2 * k_mine.shape[0], QALL), shape(F32, CHIPS, 2, QALL)),
        in_specs=[SMEM, VMEM, VMEM, VMEM],
        out_specs=(VMEM, VMEM),
        compiler_params=SMALL,
    )(position, r, k_mine, k_theirs)


def mass_kernel(stats, scores, after, out):
    tops, totals = stats[:, 0, :], stats[:, 1, :]
    top = jnp.max(tops, axis=0, keepdims=True)
    total = jnp.sum(totals * jnp.exp(tops - top), axis=0, keepdims=True)
    p = jnp.exp(scores[...] - (top + jnp.log(total)))
    kvh, local = out.shape[0] // 2, out.shape[2]
    real = (lax.broadcasted_iota(jnp.int32, (kvh, QALL), 1) < QREAL).astype(F32)
    mass = lax.dot_general(real, p, NT, precision=lax.Precision.HIGHEST, preferred_element_type=F32)
    for c in range(2):
        out[c * kvh : (c + 1) * kvh, 0, :] = mass[:, c * local : (c + 1) * local]


def mass(stats, scores, after, kvh):
    return pl.pallas_call(
        mass_kernel,
        out_shape=shape(F32, 2 * kvh, 1, scores.shape[0] // 2),
        in_specs=[VMEM, VMEM, ANY],
        out_specs=VMEM,
        compiler_params=SMALL,
    )(stats, scores, after)


def attend_kernel(e, vertical, slash, position, q, ours, theirs, *rest):
    if e:
        rest = rest[1:]
    out, token, q_buf, o_buf, k_all, v_all, sems = rest
    token[...] = jnp.zeros_like(token)
    core = position[0] & 1
    block = position[0] * 2 + e
    near = [block] + [block - jnp.where(slash[0, j] == 0, slash[0, 0], slash[0, j]) for j in range(1, NS)]
    copies = [pltpu.make_async_copy(q.at[:, pl.ds(e * BLK, BLK)], q_buf, sems.at[0])]
    copies[0].start()

    def fetch(from_ours, source, target):
        sem = sems.at[len(copies)]
        copy = pltpu.make_async_copy(source(ours), target, sem)
        other = pltpu.make_async_copy(source(theirs), target, sem)
        pl.when(from_ours)(copy.start)
        pl.when(jnp.logical_not(from_ours))(other.start)
        copies.append(copy)

    for j in range(NS):
        kept = jnp.where(near[j] >= 0, near[j], block)
        chips = (position[0] >> 1) - (kept >> 2)
        row = pl.multiple_of((kept & 1) * BLK, BLK)
        to = pl.ds(j % 2 * BLK, BLK)
        for which, target in ((0, k_all.at[j // 2, to]), (1, v_all.at[j // 2, to, pl.ds(0, HD)])):
            fetch(((kept >> 1) & 1) == core, lambda x: x.at[2 * chips + which, pl.ds(row, BLK)], target)
    to = pl.ds(NEAR, NY)
    for which, target in ((0, k_all.at[to]), (1, v_all.at[to, :, pl.ds(0, HD)])):
        fetch(core == which, lambda x: x.at[pl.ds(2 * BACK, NY)], target)
    v_all[:NEAR, :, HD:] = jnp.ones((NEAR, UNIT, HD), BF16)

    row = lax.broadcasted_iota(jnp.int32, (LISTED, HD), 0)
    drop = jnp.zeros((LISTED, HD), jnp.int32)
    for j in range(NV):
        c = vertical[0, j]
        bad = c > block
        for other in near:
            bad = bad | (c == other)
        drop = jnp.where(row // PIECE == j, bad.astype(jnp.int32), drop)
    drop = jnp.concatenate([drop.astype(F32)] * NZ, axis=0)
    keep = (1.0 - drop).astype(BF16)
    drop = drop.astype(BF16)
    for copy in copies:
        copy.wait()

    first = k_all[0, 0:1, :]
    for j in range(1, NS):

        @pl.when(near[j] < 0)
        def _(j=j):
            to = slice(j % 2 * BLK, (j % 2 + 1) * BLK)
            k_all[j // 2, to, :] = jnp.broadcast_to(first, (BLK, HD))
            v_all[j // 2, to, :] = jnp.zeros((BLK, 2 * HD), BF16)

    instead = first * drop
    for i in range(NEAR, NEAR + NY):
        k_all[i] = k_all[i] * keep + instead
        v_all[i, :, :HD] = v_all[i, :, :HD] * keep
        v_all[i, :, HD:] = keep

    factor = LOG2E / math.sqrt(HD)
    causal = lax.broadcasted_iota(jnp.int32, (BLK, BLK), 1) <= lax.broadcasted_iota(jnp.int32, (BLK, BLK), 0)
    keys = k_all[...].reshape((NV + NS) * BLK, HD)
    values = v_all[...].reshape((NV + NS) * BLK, 2 * HD)
    for h in range(0, GROUP, 2):
        n = min(2, GROUP - h)
        tile = q_buf[h : h + n].reshape(n * BLK, HD)
        s = lax.dot_general(tile, keys, NT, preferred_element_type=F32)
        own = jnp.where(jnp.concatenate([causal] * n, axis=0), s[:, :BLK], FAR)
        s = jnp.concatenate([own, s[:, BLK:]], axis=1)
        top = jnp.max(s, axis=1, keepdims=True) * factor
        w = jnp.exp2(s * factor - top).astype(BF16)
        o = jnp.dot(w, values, preferred_element_type=F32)
        o_buf[h : h + n] = (o[:, :HD] / o[:, HD:]).astype(BF16).reshape(n, BLK, HD)
    copy = pltpu.make_async_copy(o_buf, out.at[:, pl.ds(e * BLK, BLK)], sems.at[0])
    copy.start()
    copy.wait()


def attend(e, vertical, slash, position, q_t, ours, theirs, out=None):
    local = q_t.shape[1]
    args = (vertical, slash, position, q_t, ours, theirs) + ((out,) if e else ())
    return pl.pallas_call(
        functools.partial(attend_kernel, e),
        out_shape=(shape(BF16, GROUP, local, HD), shape(F32, 8, 128)),
        in_specs=[SMEM] * 3 + [ANY] * (len(args) - 3),
        out_specs=(ANY, VMEM),
        scratch_shapes=[
            pltpu.VMEM((GROUP, BLK, HD), BF16),
            pltpu.VMEM((GROUP, BLK, HD), BF16),
            pltpu.VMEM((NEAR + NY, UNIT, HD), BF16),
            pltpu.VMEM((NEAR + NY, UNIT, 2 * HD), BF16),
            pltpu.SemaphoreType.DMA((2 * NS + 3,)),
        ],
        input_output_aliases={len(args) - 1: 0} if e else {},
        compiler_params=LARGE,
        cost_estimate=pl.CostEstimate(
            flops=4 * GROUP * (NV + NS) * BLK**3, bytes_accessed=2 * 1024 * 1024, transcendentals=GROUP * (NV + NS) * BLK**2
        ),
    )(*args)


def on_device(queries, key_rows, value_rows, vertical, slash_offsets):
    local = key_rows.shape[0]
    total_len = local * NY * PER_ROW
    place = ((lax.axis_index("y") * NZ + lax.axis_index("zh")) * 2 + lax.axis_index("core")).reshape(1)
    q_t = jnp.transpose(queries, (1, 0, 2))
    k, v = key_rows[:, 0], value_rows[:, 0]

    sent, kv = pack(place, q_t, k, v)
    back = lambda x, chips: lax.ppermute(x, ("y", "zh"), [(i, (i + chips) % CHIPS) for i in range(CHIPS)])
    swap = lambda x: lax.ppermute(x, "core", [(0, 1), (1, 0)])
    k_theirs, one, three, four = swap(k), back(kv, 1), back(kv, 3), back(kv, 4)
    r = exchange(sent.reshape(2 * CHIPS, 8, HD), CTX).reshape(CHIPS, 16, HD)
    tile, again = pick(vertical, r, one, three)
    whole, again = merge(exchange(tile, "zh"), again, four, k_theirs)
    mine = exchange(whole, "y")
    scores, stats = estimate(place, mine, k, k_theirs, total_len)
    ours = together([kv, one, back(again, 1), three, four], mine)
    theirs = swap(ours)

    given = (vertical, slash_offsets, place, q_t, ours, theirs)
    out, token = attend(0, *given)
    stats = exchange(stats, ("y", "zh"))
    part = exchange(mass(stats, scores, token, lax.axis_size("kvh")), ("core", "kvh"))
    out, token = attend(1, *given, out)
    profile = jnp.sum(part, axis=(0, 1)) * (total_len / LAST / HEADS)
    return jnp.transpose(out, (1, 0, 2)), profile


def solution(mesh):
    wide = Mesh(mesh.devices.reshape(NY, NZ, 2, -1), ("y", "zh", "core", "kvh"))
    return jax.shard_map(
        on_device,
        mesh=wide,
        in_specs=(P(CTX, "kvh", None), P(CTX, "kvh", None), P(CTX, "kvh", None), P("kvh", None), P("kvh", None)),
        out_specs=(P(CTX, "kvh", None), P(CTX)),
        check_vma=False,
    )
```

```python
import functools
import math

import jax
import jax.numpy as jnp
from jax import lax
from jax.experimental import pallas as pl
from jax.experimental.pallas import tpu as pltpu
from jax.sharding import Mesh
from jax.sharding import PartitionSpec as P

BLK = 128
LAST = 64
NV = 16
NS = 8
HEADS = 40
HD = 128
GROUP = 5
FAR = -1e30
LOG2E = math.log2(math.e)
CHIP = ("y", "zhi", "zlo")
CTX = CHIP + ("core",)
NY, NZ = 8, 4
PER_ROW = 2 * NZ
CHIPS = NY * NZ
PIECES = CHIPS // 2
PIECE = BLK // PIECES
LISTED = NV * PIECE
UNIT = LISTED
NEAR = NS * BLK // UNIT
BACK = 5
QROWS = 16
QREAL = GROUP * LAST // 2
QALL = 256
NT = (((1,), (1,)), ((), ()))
SMEM = pl.BlockSpec(memory_space=pltpu.SMEM)
VMEM = pl.BlockSpec(memory_space=pltpu.VMEM)
ANY = pl.BlockSpec(memory_space=pl.ANY)
F32 = jnp.float32
BF16 = jnp.bfloat16
LARGE = pltpu.CompilerParams(vmem_limit_bytes=60 * 1024 * 1024)
MIDDLE = pltpu.CompilerParams(vmem_limit_bytes=32 * 1024 * 1024)
SMALL = pltpu.CompilerParams(vmem_limit_bytes=8 * 1024 * 1024)


def shape(kind, *dims):
    return jax.ShapeDtypeStruct(dims, kind)


def exchange(x, axis):
    return lax.all_to_all(x, axis, 0, 0)


def pack_kernel(position, q, k, v, sent, kv, last, sem):
    local = k.shape[0]
    copy = pltpu.make_async_copy(q.at[:, pl.ds(local - LAST, LAST)], last, sem)
    copy.start()

    def spread(pieces):
        for y in range(NY):
            for zhi in range(NZ // 2):
                for zlo in range(2):
                    for c in range(2):
                        sent[((y * NZ // 2 + zhi) * 2 + zlo) * 2 + c] = pieces[c][2 * y + zlo]

    cut = []
    for which, x in enumerate((k, v)):
        kv[which * local // UNIT : (which + 1) * local // UNIT] = x[...].reshape(local // UNIT, UNIT, HD)
        x = x[...].astype(F32).reshape(2, PIECES, PIECE, HD)
        cut.append(jnp.concatenate([x[0], x[1]], axis=1).astype(BF16))
    spread(cut)
    copy.wait()

    @pl.when(position[0] == 2 * CHIPS - 1)
    def _():
        flat = last[...].reshape(GROUP * LAST, HD)
        flat = jnp.concatenate([flat, jnp.zeros((2 * local - GROUP * LAST, HD), BF16)], axis=0)
        flat = flat.reshape(PIECES, 2, 2 * PIECE, HD)
        spread([flat[:, 0], flat[:, 1]])


def pack(position, q_t, k, v):
    local = k.shape[0]
    return pl.pallas_call(
        pack_kernel,
        out_shape=(shape(BF16, 2 * CHIPS, 2 * PIECE, HD), shape(BF16, 2 * local // UNIT, UNIT, HD)),
        in_specs=[SMEM, ANY, VMEM, VMEM],
        out_specs=(VMEM, VMEM),
        scratch_shapes=[pltpu.VMEM((GROUP, LAST, HD), BF16), pltpu.SemaphoreType.DMA],
        compiler_params=LARGE,
    )(position, q_t, k, v)


def choose_kernel(ids, out):
    wanted, given = out.shape
    row = lax.broadcasted_iota(jnp.int32, (wanted, HD), 0)
    source = given - wanted + row
    for j in range(NV):
        source = jnp.where(row // PIECE == j, ids[0, j] * PIECE + row % PIECE, source)
    column = lax.broadcasted_iota(jnp.int32, (wanted, HD), 1)
    for i in range(0, given, HD):
        out[:, i : i + HD] = (column + i == source).astype(F32).astype(BF16)


def choose(vertical):
    return pl.pallas_call(
        choose_kernel,
        out_shape=shape(BF16, LISTED + QROWS, 4 * CHIPS * PIECE),
        in_specs=[SMEM],
        out_specs=VMEM,
        compiler_params=SMALL,
    )(vertical)


def pick_kernel(chosen, r, one, three, out):
    rows = r[...].reshape(4 * CHIPS * PIECE, HD)
    tile = jnp.dot(chosen[...], rows, preferred_element_type=F32).astype(BF16)
    for d in range(PIECES):
        out[d] = tile


def pick(chosen, r, one, three):
    return pl.pallas_call(
        pick_kernel,
        out_shape=shape(BF16, PIECES, LISTED + QROWS, HD),
        in_specs=[VMEM, VMEM, ANY, ANY],
        out_specs=VMEM,
        compiler_params=SMALL,
    )(chosen, r, one, three)


def together_kernel(*refs):
    *parts, mine, after, out, sems = refs
    n = len(parts)
    each = parts[0].shape[0]
    copies = [pltpu.make_async_copy(part, out.at[pl.ds(each * i, each)], sems.at[i]) for i, part in enumerate(parts)]
    copies.append(pltpu.make_async_copy(mine.at[:, pl.ds(0, LISTED)], out.at[pl.ds(each * n, PIECES)], sems.at[n]))
    for copy in copies:
        copy.start()
    for copy in copies:
        copy.wait()


def together(parts, mine, after):
    n = len(parts)
    return pl.pallas_call(
        together_kernel,
        out_shape=shape(BF16, n * parts[0].shape[0] + PIECES, UNIT, HD),
        in_specs=[ANY] * (n + 2),
        out_specs=ANY,
        scratch_shapes=[pltpu.SemaphoreType.DMA((n + 1,))],
        compiler_params=SMALL,
    )(*parts, mine, after)


def estimate_kernel(total_len, position, q, k_mine, k_theirs, scores, stats):
    tokens = 2 * k_mine.shape[0]
    core = position[0] & 1
    mine, theirs = k_mine[...], k_theirs[...]
    k = jnp.concatenate([jnp.where(core == 0, mine, theirs), jnp.where(core == 0, theirs, mine)], axis=0)
    s = lax.dot_general(k, q[...], NT, preferred_element_type=F32) * (1.0 / math.sqrt(HD))
    column = lax.broadcasted_iota(jnp.int32, (1, QALL), 1)
    last_pos = total_len - LAST + ((column >> 4) * 32 + core * 16 + (column & 15)) % LAST
    key_pos = (position[0] >> 1) * tokens + lax.broadcasted_iota(jnp.int32, (tokens, QALL), 0)
    s = jnp.where(key_pos <= last_pos, s, FAR)
    scores[...] = s
    top = jnp.max(s, axis=0, keepdims=True)
    total = jnp.sum(jnp.exp(s - top), axis=0, keepdims=True)
    both = jnp.concatenate([top, total], axis=0)
    for d in range(CHIPS):
        stats[d] = both


def estimate(position, q, k_mine, k_theirs, total_len):
    return pl.pallas_call(
        functools.partial(estimate_kernel, total_len),
        out_shape=(shape(F32, 2 * k_mine.shape[0], QALL), shape(F32, CHIPS, 2, QALL)),
        in_specs=[SMEM, VMEM, VMEM, VMEM],
        out_specs=(VMEM, VMEM),
        compiler_params=SMALL,
    )(position, q, k_mine, k_theirs)


def mass_kernel(factor, stats, scores, after, out):
    tops, totals = stats[:, 0, :], stats[:, 1, :]
    top = jnp.max(tops, axis=0, keepdims=True)
    total = jnp.sum(totals * jnp.exp(tops - top), axis=0, keepdims=True)
    p = jnp.exp(scores[...] - (top + jnp.log(total)))
    kvh, local = out.shape[0] // 2, out.shape[2]
    real = (lax.broadcasted_iota(jnp.int32, (kvh, QALL), 1) < QREAL).astype(BF16)
    high = p.astype(BF16)
    low = (p - high.astype(F32)).astype(BF16)
    mass = sum(lax.dot_general(real, x, NT, preferred_element_type=F32) for x in (high, low)) * factor
    for c in range(2):
        out[c * kvh : (c + 1) * kvh, 0, :] = mass[:, c * local : (c + 1) * local]


def mass(stats, scores, after, kvh, factor):
    return pl.pallas_call(
        functools.partial(mass_kernel, factor),
        out_shape=shape(F32, 2 * kvh, 1, scores.shape[0] // 2),
        in_specs=[VMEM, VMEM, ANY],
        out_specs=VMEM,
        compiler_params=SMALL,
    )(stats, scores, after)


def attend_kernel(e, vertical, slash, position, q, ours, theirs, *rest):
    if e:
        rest = rest[1:]
    out, token, q_buf, o_buf, k_all, v_all, sems = rest
    token[...] = jnp.zeros_like(token)
    core = position[0] & 1
    block = position[0] * 2 + e
    near = [block] + [block - jnp.where(slash[0, j] == 0, slash[0, 0], slash[0, j]) for j in range(1, NS)]
    copies = [pltpu.make_async_copy(q.at[:, pl.ds(e * BLK, BLK)], q_buf, sems.at[0])]
    copies[0].start()

    def fetch(from_ours, source, target):
        sem = sems.at[len(copies)]
        copy = pltpu.make_async_copy(source(ours), target, sem)
        other = pltpu.make_async_copy(source(theirs), target, sem)
        pl.when(from_ours)(copy.start)
        pl.when(jnp.logical_not(from_ours))(other.start)
        copies.append(copy)

    per = BLK // UNIT
    for j in range(NS):
        kept = jnp.where(near[j] >= 0, near[j], block)
        chips = (position[0] >> 1) - (kept >> 2)
        to = pl.ds(j * per, per)
        for which, target in ((0, k_all.at[to]), (1, v_all.at[to, :, pl.ds(0, HD)])):
            unit = (2 * chips + which) * 2 * per + (kept & 1) * per
            fetch(((kept >> 1) & 1) == core, lambda x: x.at[pl.ds(unit, per)], target)
    v_all[:NEAR, :, HD:] = jnp.ones((NEAR, UNIT, HD), BF16)

    row = lax.broadcasted_iota(jnp.int32, (UNIT, HD), 0)
    drop = jnp.zeros((UNIT, HD), jnp.int32)
    for j in range(NV):
        c = vertical[0, j]
        bad = c > block
        for other in near:
            bad = bad | (c == other)
        drop = jnp.where(row // PIECE == j, bad.astype(jnp.int32), drop)
    drop = drop.astype(F32)
    keep = (1.0 - drop).astype(BF16)
    drop = drop.astype(BF16)
    first = ours[e * per, 0:1, :]
    instead = first * drop
    listed = ours.shape[0] - PIECES
    for c, (k, v) in enumerate(((ours, theirs), (theirs, ours))):

        @pl.when(core == c)
        def _(k=k, v=v):
            for i in range(PIECES):
                k_all[NEAR + i] = k[listed + i] * keep + instead
                v_all[NEAR + i, :, :HD] = v[listed + i] * keep

    for i in range(PIECES):
        v_all[NEAR + i, :, HD:] = keep
    for copy in copies:
        copy.wait()
    for j in range(1, NS):

        @pl.when(near[j] < 0)
        def _(j=j):
            to = slice(j * per, (j + 1) * per)
            k_all[to] = jnp.broadcast_to(first, (per, UNIT, HD))
            v_all[to] = jnp.zeros((per, UNIT, 2 * HD), BF16)

    factor = LOG2E / math.sqrt(HD)
    causal = lax.broadcasted_iota(jnp.int32, (BLK, BLK), 1) <= lax.broadcasted_iota(jnp.int32, (BLK, BLK), 0)
    keys = k_all[...].reshape((NV + NS) * BLK, HD)
    values = v_all[...].reshape((NV + NS) * BLK, 2 * HD)
    pair = 2

    def score(h):
        n = min(pair, GROUP - h)
        tile = q_buf[h : h + n].reshape(n * BLK, HD)
        s = lax.dot_general(tile, keys, NT, preferred_element_type=F32)
        own = jnp.where(jnp.concatenate([causal] * n, axis=0), s[:, :BLK], FAR)
        s = jnp.concatenate([own, s[:, BLK:]], axis=1)
        return s, jnp.max(s, axis=1, keepdims=True) * factor

    def finish(h, s, top):
        n = min(pair, GROUP - h)
        w = jnp.exp2(s * factor - top).astype(BF16)
        o = jnp.dot(w, values, preferred_element_type=F32)
        o_buf[h : h + n] = (o[:, :HD] / o[:, HD:]).astype(BF16).reshape(n, BLK, HD)
        copies.append(pltpu.make_async_copy(o_buf.at[pl.ds(h, n)], out.at[pl.ds(h, n), pl.ds(e * BLK, BLK)], sems.at[h]))
        copies[-1].start()

    held = score(0)
    for h in range(0, GROUP, pair):
        later = score(h + pair) if h + pair < GROUP else None
        finish(h, *held)
        held = later
    for copy in copies[2 * NS + 1 :]:
        copy.wait()


def attend(e, vertical, slash, position, q_t, ours, theirs, out=None):
    local = q_t.shape[1]
    args = (vertical, slash, position, q_t, ours, theirs) + ((out,) if e else ())
    return pl.pallas_call(
        functools.partial(attend_kernel, e),
        out_shape=(shape(BF16, GROUP, local, HD), shape(F32, 8, 128)),
        in_specs=[SMEM] * 3 + [ANY, VMEM, VMEM] + [ANY] * (len(args) - 6),
        out_specs=(ANY, VMEM),
        scratch_shapes=[
            pltpu.VMEM((GROUP, BLK, HD), BF16),
            pltpu.VMEM((GROUP, BLK, HD), BF16),
            pltpu.VMEM((NEAR + PIECES, UNIT, HD), BF16),
            pltpu.VMEM((NEAR + PIECES, UNIT, 2 * HD), BF16),
            pltpu.SemaphoreType.DMA((2 * NS + 1,)),
        ],
        input_output_aliases={len(args) - 1: 0} if e else {},
        compiler_params=MIDDLE,
        cost_estimate=pl.CostEstimate(
            flops=4 * GROUP * (NV + NS) * BLK**3, bytes_accessed=2 * 1024 * 1024, transcendentals=GROUP * (NV + NS) * BLK**2
        ),
    )(*args)


def on_device(queries, key_rows, value_rows, vertical, slash_offsets):
    local = key_rows.shape[0]
    total_len = local * NY * PER_ROW
    place = lax.axis_index(CTX).reshape(1)
    q_t = jnp.transpose(queries, (1, 0, 2))
    k, v = key_rows[:, 0], value_rows[:, 0]

    sent, kv = pack(place, q_t, k, v)
    back = lambda x, chips: lax.ppermute(x, CHIP, [(i, (i + chips) % CHIPS) for i in range(CHIPS)])
    swap = lambda x: lax.ppermute(x, "core", [(0, 1), (1, 0)])
    one, three = back(kv, 1), back(kv, 3)
    r = exchange(sent, CTX)
    mine = exchange(pick(choose(vertical), r, one, three), ("y", "zlo"))
    k_theirs, two, four = swap(k), back(three, -1), back(kv, 4)
    scores, stats = estimate(place, mine[:, LISTED:].reshape(QALL, HD), k, k_theirs, total_len)
    ours = together([kv, one, two, three, four], mine, k_theirs)
    theirs = swap(ours)

    given = (vertical, slash_offsets, place, q_t, ours, theirs)
    out, token = attend(0, *given)
    stats = exchange(stats, CHIP)
    part = exchange(mass(stats, scores, token, lax.axis_size("kvh"), total_len / LAST / HEADS), ("core", "kvh"))
    out, token = attend(1, *given, out)
    profile = jnp.sum(part, axis=(0, 1))
    return jnp.transpose(out, (1, 0, 2)), profile


def solution(mesh):
    wide = Mesh(mesh.devices.reshape(NY, NZ // 2, 2, 2, -1), CTX + ("kvh",))
    return jax.shard_map(
        on_device,
        mesh=wide,
        in_specs=(P(CTX, "kvh", None), P(CTX, "kvh", None), P(CTX, "kvh", None), P("kvh", None), P("kvh", None)),
        out_specs=(P(CTX, "kvh", None), P(CTX)),
        check_vma=False,
    )
```

```python
import functools
import math

import jax
import jax.numpy as jnp
from jax import lax
from jax.experimental import pallas as pl
from jax.experimental.pallas import tpu as pltpu
from jax.sharding import Mesh
from jax.sharding import PartitionSpec as P

BLK = 128
LAST = 64
NV = 16
NS = 8
HEADS = 40
HD = 128
GROUP = 5
FAR = -1e30
LOG2E = math.log2(math.e)
CHIP = ("y", "zhi", "zlo")
CTX = CHIP + ("core",)
NY, NZ = 8, 4
PER_ROW = 2 * NZ
CHIPS = NY * NZ
PIECES = CHIPS // 2
PIECE = BLK // PIECES
LISTED = NV * PIECE
UNIT = LISTED
NEAR = NS * BLK // UNIT
BACK = 5
QROWS = 16
QREAL = GROUP * LAST // 2
QALL = 256
NT = (((1,), (1,)), ((), ()))
SMEM = pl.BlockSpec(memory_space=pltpu.SMEM)
VMEM = pl.BlockSpec(memory_space=pltpu.VMEM)
ANY = pl.BlockSpec(memory_space=pl.ANY)
HBM = pl.BlockSpec(memory_space=pltpu.HBM)
F32 = jnp.float32
BF16 = jnp.bfloat16
LARGE = pltpu.CompilerParams(vmem_limit_bytes=60 * 1024 * 1024)
MIDDLE = pltpu.CompilerParams(vmem_limit_bytes=32 * 1024 * 1024)
SMALL = pltpu.CompilerParams(vmem_limit_bytes=8 * 1024 * 1024)


def shape(kind, *dims):
    return jax.ShapeDtypeStruct(dims, kind)


def exchange(x, axis):
    return lax.all_to_all(x, axis, 0, 0)


def pack_kernel(position, q, k, v, sent, kv, last, sem):
    local = k.shape[0]
    copy = pltpu.make_async_copy(q.at[:, pl.ds(local - LAST, LAST)], last, sem)
    copy.start()

    def spread(pieces):
        for y in range(NY):
            for zhi in range(NZ // 2):
                for zlo in range(2):
                    for c in range(2):
                        sent[((y * NZ // 2 + zhi) * 2 + zlo) * 2 + c] = pieces[c][2 * y + zlo]

    cut = []
    for which, x in enumerate((k, v)):
        kv[which * local // UNIT : (which + 1) * local // UNIT] = x[...].reshape(local // UNIT, UNIT, HD)
        x = x[...].astype(F32).reshape(2, PIECES, PIECE, HD)
        cut.append(jnp.concatenate([x[0], x[1]], axis=1).astype(BF16))
    spread(cut)
    copy.wait()

    @pl.when(position[0] == 2 * CHIPS - 1)
    def _():
        flat = last[...].reshape(GROUP * LAST, HD)
        flat = jnp.concatenate([flat, jnp.zeros((2 * local - GROUP * LAST, HD), BF16)], axis=0)
        flat = flat.reshape(PIECES, 2, 2 * PIECE, HD)
        spread([flat[:, 0], flat[:, 1]])


def pack(position, q_t, k, v):
    local = k.shape[0]
    return pl.pallas_call(
        pack_kernel,
        out_shape=(shape(BF16, 2 * CHIPS, 2 * PIECE, HD), shape(BF16, 2 * local // UNIT, UNIT, HD)),
        in_specs=[SMEM, ANY, VMEM, VMEM],
        out_specs=(VMEM, VMEM),
        scratch_shapes=[pltpu.VMEM((GROUP, LAST, HD), BF16), pltpu.SemaphoreType.DMA],
        compiler_params=LARGE,
    )(position, q_t, k, v)


def choose_kernel(ids, out):
    wanted, given = out.shape
    row = lax.broadcasted_iota(jnp.int32, (wanted, HD), 0)
    source = given - wanted + row
    for j in range(NV):
        source = jnp.where(row // PIECE == j, ids[0, j] * PIECE + row % PIECE, source)
    column = lax.broadcasted_iota(jnp.int32, (wanted, HD), 1)
    for i in range(0, given, HD):
        out[:, i : i + HD] = (column + i == source).astype(F32).astype(BF16)


def choose(vertical):
    return pl.pallas_call(
        choose_kernel,
        out_shape=shape(BF16, LISTED + QROWS, 4 * CHIPS * PIECE),
        in_specs=[SMEM],
        out_specs=VMEM,
        compiler_params=SMALL,
    )(vertical)


def pick_kernel(chosen, r, three, four, k_theirs, out):
    rows = r[...].reshape(4 * CHIPS * PIECE, HD)
    tile = jnp.dot(chosen[...], rows, preferred_element_type=F32).astype(BF16)
    for d in range(PIECES):
        out[d] = tile


def pick(chosen, r, three, four, k_theirs):
    return pl.pallas_call(
        pick_kernel,
        out_shape=shape(BF16, PIECES, LISTED + QROWS, HD),
        in_specs=[VMEM, VMEM, ANY, ANY, ANY],
        out_specs=VMEM,
        compiler_params=SMALL,
    )(chosen, r, three, four, k_theirs)


def together_kernel(*refs):
    *parts, mine, after, out, sems = refs
    n = len(parts)
    each = parts[0].shape[0]
    copies = [pltpu.make_async_copy(part, out.at[pl.ds(each * i, each)], sems.at[i]) for i, part in enumerate(parts)]
    copies.append(pltpu.make_async_copy(mine.at[:, pl.ds(0, LISTED)], out.at[pl.ds(each * n, PIECES)], sems.at[n]))
    for copy in copies:
        copy.start()
    for copy in copies:
        copy.wait()


def together(parts, mine, after):
    n = len(parts)
    return pl.pallas_call(
        together_kernel,
        out_shape=shape(BF16, n * parts[0].shape[0] + PIECES, UNIT, HD),
        in_specs=[ANY] * (n + 2),
        out_specs=ANY,
        scratch_shapes=[pltpu.SemaphoreType.DMA((n + 1,))],
        compiler_params=SMALL,
    )(*parts, mine, after)


def estimate_kernel(total_len, position, q, k_mine, k_theirs, scores, stats):
    tokens = 2 * k_mine.shape[0]
    core = position[0] & 1
    mine, theirs = k_mine[...], k_theirs[...]
    k = jnp.concatenate([jnp.where(core == 0, mine, theirs), jnp.where(core == 0, theirs, mine)], axis=0)
    s = lax.dot_general(k, q[...], NT, preferred_element_type=F32) * (1.0 / math.sqrt(HD))
    column = lax.broadcasted_iota(jnp.int32, (1, QALL), 1)
    last_pos = total_len - LAST + ((column >> 4) * 32 + core * 16 + (column & 15)) % LAST
    key_pos = (position[0] >> 1) * tokens + lax.broadcasted_iota(jnp.int32, (tokens, QALL), 0)
    s = jnp.where(key_pos <= last_pos, s, FAR)
    scores[...] = s
    top = jnp.max(s, axis=0, keepdims=True)
    total = jnp.sum(jnp.exp(s - top), axis=0, keepdims=True)
    both = jnp.concatenate([top, total], axis=0)
    for d in range(CHIPS):
        stats[d] = both


def estimate(position, q, k_mine, k_theirs, total_len):
    return pl.pallas_call(
        functools.partial(estimate_kernel, total_len),
        out_shape=(shape(F32, 2 * k_mine.shape[0], QALL), shape(F32, CHIPS, 2, QALL)),
        in_specs=[SMEM, VMEM, VMEM, VMEM],
        out_specs=(VMEM, VMEM),
        compiler_params=SMALL,
    )(position, q, k_mine, k_theirs)


def mass_kernel(factor, stats, scores, after, out):
    tops, totals = stats[:, 0, :], stats[:, 1, :]
    top = jnp.max(tops, axis=0, keepdims=True)
    total = jnp.sum(totals * jnp.exp(tops - top), axis=0, keepdims=True)
    p = jnp.exp(scores[...] - (top + jnp.log(total)))
    kvh, local = out.shape[0] // 2, out.shape[2]
    real = (lax.broadcasted_iota(jnp.int32, (kvh, QALL), 1) < QREAL).astype(BF16)
    high = p.astype(BF16)
    low = (p - high.astype(F32)).astype(BF16)
    mass = sum(lax.dot_general(real, x, NT, preferred_element_type=F32) for x in (high, low)) * factor
    for c in range(2):
        out[c * kvh : (c + 1) * kvh, 0, :] = mass[:, c * local : (c + 1) * local]


def mass(stats, scores, after, kvh, factor):
    return pl.pallas_call(
        functools.partial(mass_kernel, factor),
        out_shape=shape(F32, 2 * kvh, 1, scores.shape[0] // 2),
        in_specs=[VMEM, VMEM, ANY],
        out_specs=VMEM,
        compiler_params=SMALL,
    )(stats, scores, after)


def block_numbers(e, slash, position):
    block = position[0] * 2 + e
    return [block] + [block - jnp.where(slash[0, j] == 0, slash[0, 0], slash[0, j]) for j in range(1, NS)]


def fetch(near, core, position, ours, theirs, k_all, v_all, sems):
    per = BLK // UNIT
    copies = []
    for j in range(NS):
        kept = jnp.where(near[j] >= 0, near[j], near[0])
        chips = (position[0] >> 1) - (kept >> 2)
        to = pl.ds(j * per, per)
        for which, target in ((0, k_all.at[to]), (1, v_all.at[to, :, pl.ds(0, HD)])):
            unit = (2 * chips + which) * 2 * per + (kept & 1) * per
            copy = pltpu.make_async_copy(ours.at[pl.ds(unit, per)], target, sems.at[len(copies)])
            other = pltpu.make_async_copy(theirs.at[pl.ds(unit, per)], target, sems.at[len(copies)])
            from_ours = ((kept >> 1) & 1) == core
            pl.when(from_ours)(copy.start)
            pl.when(jnp.logical_not(from_ours))(other.start)
            copies.append(copy)
    return copies


def fill(e, near, core, vertical, ours, theirs, k_all, v_all, copies):
    per = BLK // UNIT
    row = lax.broadcasted_iota(jnp.int32, (UNIT, HD), 0)
    drop = jnp.zeros((UNIT, HD), jnp.int32)
    for j in range(NV):
        c = vertical[0, j]
        bad = c > near[0]
        for other in near:
            bad = bad | (c == other)
        drop = jnp.where(row // PIECE == j, bad.astype(jnp.int32), drop)
    drop = drop.astype(F32)
    keep = (1.0 - drop).astype(BF16)
    first = ours[e * per, 0:1, :]
    instead = first * drop.astype(BF16)
    listed = ours.shape[0] - PIECES
    for c, (k, v) in enumerate(((ours, theirs), (theirs, ours))):

        @pl.when(core == c)
        def _(k=k, v=v):
            for i in range(PIECES):
                k_all[NEAR + i] = k[listed + i] * keep + instead
                v_all[NEAR + i, :, :HD] = v[listed + i] * keep

    for copy in copies:
        copy.wait()
    for j in range(1, NS):

        @pl.when(near[j] < 0)
        def _(j=j):
            to = slice(j * per, (j + 1) * per)
            k_all[to] = jnp.broadcast_to(first, (per, UNIT, HD))
            v_all[to, :, :HD] = jnp.zeros((per, UNIT, HD), BF16)

    counts = [jnp.where(near[j // per] >= 0, jnp.ones((UNIT, HD), F32), 0.0).astype(BF16) for j in range(NEAR)]
    return counts + [keep]


def count(v_all, counts):
    for j in range(NEAR):
        v_all[j, :, HD:] = counts[j]
    for i in range(NEAR, NEAR + PIECES):
        v_all[i, :, HD:] = counts[NEAR]


def heads(e, q_buf, o_buf, k_all, v_all, out, sems):
    factor = LOG2E / math.sqrt(HD)
    causal = lax.broadcasted_iota(jnp.int32, (BLK, BLK), 1) <= lax.broadcasted_iota(jnp.int32, (BLK, BLK), 0)
    keys = k_all[...].reshape((NV + NS) * BLK, HD)
    values = v_all[...].reshape((NV + NS) * BLK, 2 * HD)
    pair = 2
    copies = []

    def score(h):
        n = min(pair, GROUP - h)
        tile = q_buf[h : h + n].reshape(n * BLK, HD)
        s = lax.dot_general(tile, keys, NT, preferred_element_type=F32)
        own = jnp.where(jnp.concatenate([causal] * n, axis=0), s[:, :BLK], FAR)
        s = jnp.concatenate([own, s[:, BLK:]], axis=1)
        return s, jnp.max(s, axis=1, keepdims=True) * factor

    def finish(h, s, top):
        n = min(pair, GROUP - h)
        w = jnp.exp2(s * factor - top).astype(BF16)
        o = jnp.dot(w, values, preferred_element_type=F32)
        o_buf[h : h + n] = (o[:, :HD] / o[:, HD:]).astype(BF16).reshape(n, BLK, HD)
        copies.append(pltpu.make_async_copy(o_buf.at[pl.ds(h, n)], out.at[pl.ds(h, n), pl.ds(e * BLK, BLK)], sems.at[h]))
        copies[-1].start()

    held = score(0)
    for h in range(0, GROUP, pair):
        later = score(h + pair) if h + pair < GROUP else None
        finish(h, *held)
        held = later
    return copies


def first_kernel(vertical, slash, position, q, ours, theirs, out, ours_next, theirs_next, token, q_buf, o_buf, k_all, v_all, k_next, v_next, sems, near_sems, next_sems):
    token[...] = jnp.zeros_like(token)
    core = position[0] & 1
    copy = pltpu.make_async_copy(q.at[:, pl.ds(0, BLK)], q_buf, sems.at[0])
    copy.start()
    near = block_numbers(0, slash, position)
    copies = fetch(near, core, position, ours, theirs, k_all, v_all, near_sems)
    near_next = block_numbers(1, slash, position)
    copies_next = fetch(near_next, core, position, ours, theirs, k_next, v_next, next_sems)
    count(v_all, fill(0, near, core, vertical, ours, theirs, k_all, v_all, copies))
    copy.wait()
    written = heads(0, q_buf, o_buf, k_all, v_all, out, sems)
    counts = fill(1, near_next, core, vertical, ours, theirs, k_next, v_next, copies_next)
    n = NEAR + PIECES
    ours_next[:n] = k_next[...]
    theirs_next[:n] = v_next[...]
    for j, x in enumerate(counts):
        ours_next[n + j] = x
    for copy in written:
        copy.wait()


def second_kernel(q, ours, theirs, before, out, q_buf, o_buf, v_all, sems):
    n = NEAR + PIECES
    copy = pltpu.make_async_copy(q.at[:, pl.ds(BLK, BLK)], q_buf, sems.at[0])
    copy.start()
    v_all[:, :, :HD] = theirs[:n]
    count(v_all, [ours[n + j] for j in range(NEAR + 1)])
    copy.wait()
    for copy in heads(1, q_buf, o_buf, ours.at[pl.ds(0, n)], v_all, out, sems):
        copy.wait()


COST = pl.CostEstimate(flops=4 * GROUP * (NV + NS) * BLK**3, bytes_accessed=2 * 1024 * 1024, transcendentals=GROUP * (NV + NS) * BLK**2)
KEYS = (NEAR + PIECES, UNIT, HD)
VALUES = (NEAR + PIECES, UNIT, 2 * HD)
TILE = (GROUP, BLK, HD)


def attend_first(vertical, slash, position, q_t, ours, theirs):
    return pl.pallas_call(
        first_kernel,
        out_shape=(shape(BF16, *q_t.shape), shape(BF16, *ours.shape), shape(BF16, *ours.shape), shape(F32, 8, 128)),
        in_specs=[SMEM] * 3 + [HBM, VMEM, VMEM],
        out_specs=(ANY, VMEM, VMEM, VMEM),
        input_output_aliases={4: 1, 5: 2},
        scratch_shapes=[
            pltpu.VMEM(TILE, BF16),
            pltpu.VMEM(TILE, BF16),
            pltpu.VMEM(KEYS, BF16),
            pltpu.VMEM(VALUES, BF16),
            pltpu.VMEM(KEYS, BF16),
            pltpu.VMEM(KEYS, BF16),
            pltpu.SemaphoreType.DMA((GROUP,)),
            pltpu.SemaphoreType.DMA((2 * NS,)),
            pltpu.SemaphoreType.DMA((2 * NS,)),
        ],
        compiler_params=MIDDLE,
        cost_estimate=COST,
    )(vertical, slash, position, q_t, ours, theirs)


def attend_second(q_t, ours, theirs, out):
    return pl.pallas_call(
        second_kernel,
        out_shape=shape(BF16, *q_t.shape),
        in_specs=[HBM, VMEM, VMEM, ANY],
        out_specs=ANY,
        scratch_shapes=[pltpu.VMEM(TILE, BF16), pltpu.VMEM(TILE, BF16), pltpu.VMEM(VALUES, BF16), pltpu.SemaphoreType.DMA((GROUP,))],
        input_output_aliases={3: 0},
        compiler_params=MIDDLE,
        cost_estimate=COST,
    )(q_t, ours, theirs, out)


def on_device(queries, key_rows, value_rows, vertical, slash_offsets):
    local = key_rows.shape[0]
    total_len = local * NY * PER_ROW
    place = lax.axis_index(CTX).reshape(1)
    q_t = jnp.transpose(queries, (1, 0, 2))
    k, v = key_rows[:, 0], value_rows[:, 0]

    sent, kv = pack(place, q_t, k, v)
    back = lambda x, chips: lax.ppermute(x, CHIP, [(i, (i + chips) % CHIPS) for i in range(CHIPS)])
    swap = lambda x: lax.ppermute(x, "core", [(0, 1), (1, 0)])
    three, four, k_theirs = back(kv, 3), back(kv, 4), swap(k)
    r = exchange(sent, CTX)
    mine = exchange(pick(choose(vertical), r, three, four, k_theirs), ("y", "zlo"))
    one, two = back(kv, 1), back(three, -1)
    scores, stats = estimate(place, mine[:, LISTED:].reshape(QALL, HD), k, k_theirs, total_len)
    ours = together([kv, one, two, three, four], mine, scores)
    theirs = swap(ours)

    out, ours, theirs, token = attend_first(vertical, slash_offsets, place, q_t, ours, theirs)
    stats = exchange(stats, CHIP)
    part = exchange(mass(stats, scores, token, lax.axis_size("kvh"), total_len / LAST / HEADS), ("core", "kvh"))
    out = attend_second(q_t, ours, theirs, out)
    profile = jnp.sum(part, axis=(0, 1))
    return jnp.transpose(out, (1, 0, 2)), profile


def solution(mesh):
    wide = Mesh(mesh.devices.reshape(NY, NZ // 2, 2, 2, -1), CTX + ("kvh",))
    return jax.shard_map(
        on_device,
        mesh=wide,
        in_specs=(P(CTX, "kvh", None), P(CTX, "kvh", None), P(CTX, "kvh", None), P("kvh", None), P("kvh", None)),
        out_specs=(P(CTX, "kvh", None), P(CTX)),
        check_vma=False,
    )
```

```python
import functools
import math

import jax
import jax.numpy as jnp
from jax import lax
from jax.experimental import pallas as pl
from jax.experimental.pallas import tpu as pltpu
from jax.sharding import Mesh
from jax.sharding import PartitionSpec as P

BLK = 128
LAST = 64
NV = 16
NS = 8
HEADS = 40
HD = 128
GROUP = 5
FAR = -1e30
LOG2E = math.log2(math.e)
CHIP = ("y", "zhi", "zlo")
CTX = CHIP + ("core",)
NY, NZ = 8, 4
PER_ROW = 2 * NZ
CHIPS = NY * NZ
PIECES = CHIPS // 2
PIECE = BLK // PIECES
LISTED = NV * PIECE
UNIT = LISTED
NEAR = NS * BLK // UNIT
BACK = 5
QROWS = 16
QREAL = GROUP * LAST // 2
QALL = 256
NT = (((1,), (1,)), ((), ()))
SMEM = pl.BlockSpec(memory_space=pltpu.SMEM)
VMEM = pl.BlockSpec(memory_space=pltpu.VMEM)
ANY = pl.BlockSpec(memory_space=pl.ANY)
HBM = pl.BlockSpec(memory_space=pltpu.HBM)
F32 = jnp.float32
BF16 = jnp.bfloat16
LARGE = pltpu.CompilerParams(vmem_limit_bytes=60 * 1024 * 1024)
MIDDLE = pltpu.CompilerParams(vmem_limit_bytes=32 * 1024 * 1024)
SMALL = pltpu.CompilerParams(vmem_limit_bytes=8 * 1024 * 1024)


def shape(kind, *dims):
    return jax.ShapeDtypeStruct(dims, kind)


def exchange(x, axis):
    return lax.all_to_all(x, axis, 0, 0)


def pack_kernel(position, q, k, v, sent, kv, last, sem):
    local = k.shape[0]
    copy = pltpu.make_async_copy(q.at[:, pl.ds(local - LAST, LAST)], last, sem)
    copy.start()

    def spread(pieces):
        for y in range(NY):
            for zhi in range(NZ // 2):
                for zlo in range(2):
                    for c in range(2):
                        sent[((y * NZ // 2 + zhi) * 2 + zlo) * 2 + c] = pieces[c][2 * y + zlo]

    cut = []
    for which, x in enumerate((k, v)):
        kv[which * local // UNIT : (which + 1) * local // UNIT] = x[...].reshape(local // UNIT, UNIT, HD)
        x = x[...].astype(F32).reshape(2, PIECES, PIECE, HD)
        cut.append(jnp.concatenate([x[0], x[1]], axis=1).astype(BF16))
    spread(cut)
    copy.wait()

    @pl.when(position[0] == 2 * CHIPS - 1)
    def _():
        flat = last[...].reshape(GROUP * LAST, HD)
        flat = jnp.concatenate([flat, jnp.zeros((2 * local - GROUP * LAST, HD), BF16)], axis=0)
        flat = flat.reshape(PIECES, 2, 2 * PIECE, HD)
        spread([flat[:, 0], flat[:, 1]])


def pack(position, q_t, k, v):
    local = k.shape[0]
    return pl.pallas_call(
        pack_kernel,
        out_shape=(shape(BF16, 2 * CHIPS, 2 * PIECE, HD), shape(BF16, 2 * local // UNIT, UNIT, HD)),
        in_specs=[SMEM, ANY, VMEM, VMEM],
        out_specs=(VMEM, VMEM),
        scratch_shapes=[pltpu.VMEM((GROUP, LAST, HD), BF16), pltpu.SemaphoreType.DMA],
        compiler_params=LARGE,
    )(position, q_t, k, v)


def choose_kernel(ids, out):
    wanted, given = out.shape
    row = lax.broadcasted_iota(jnp.int32, (wanted, HD), 0)
    source = given - wanted + row
    for j in range(NV):
        source = jnp.where(row // PIECE == j, ids[0, j] * PIECE + row % PIECE, source)
    column = lax.broadcasted_iota(jnp.int32, (wanted, HD), 1)
    for i in range(0, given, HD):
        out[:, i : i + HD] = (column + i == source).astype(F32).astype(BF16)


def choose(vertical):
    return pl.pallas_call(
        choose_kernel,
        out_shape=shape(BF16, LISTED + QROWS, 4 * CHIPS * PIECE),
        in_specs=[SMEM],
        out_specs=VMEM,
        compiler_params=SMALL,
    )(vertical)


def pick_kernel(chosen, r, three, k_theirs, out):
    rows = r[...].reshape(4 * CHIPS * PIECE, HD)
    tile = jnp.dot(chosen[...], rows, preferred_element_type=F32).astype(BF16)
    for d in range(PIECES):
        out[d] = tile


def pick(chosen, r, three, k_theirs):
    return pl.pallas_call(
        pick_kernel,
        out_shape=shape(BF16, PIECES, LISTED + QROWS, HD),
        in_specs=[VMEM, VMEM, ANY, ANY],
        out_specs=VMEM,
        compiler_params=SMALL,
    )(chosen, r, three, k_theirs)


def together_kernel(*refs):
    *parts, mine, after, out, sems = refs
    n = len(parts)
    each = parts[0].shape[0]
    copies = [pltpu.make_async_copy(part, out.at[pl.ds(each * i, each)], sems.at[i]) for i, part in enumerate(parts)]
    copies.append(pltpu.make_async_copy(mine.at[:, pl.ds(0, LISTED)], out.at[pl.ds(each * n, PIECES)], sems.at[n]))
    for copy in copies:
        copy.start()
    for copy in copies:
        copy.wait()


def together(parts, mine, after):
    n = len(parts)
    return pl.pallas_call(
        together_kernel,
        out_shape=shape(BF16, n * parts[0].shape[0] + PIECES, UNIT, HD),
        in_specs=[ANY] * (n + 2),
        out_specs=ANY,
        scratch_shapes=[pltpu.SemaphoreType.DMA((n + 1,))],
        compiler_params=SMALL,
    )(*parts, mine, after)


def estimate_kernel(total_len, position, q, k_mine, k_theirs, scores, stats):
    tokens = 2 * k_mine.shape[0]
    core = position[0] & 1
    mine, theirs = k_mine[...], k_theirs[...]
    k = jnp.concatenate([jnp.where(core == 0, mine, theirs), jnp.where(core == 0, theirs, mine)], axis=0)
    s = lax.dot_general(k, q[...], NT, preferred_element_type=F32) * (1.0 / math.sqrt(HD))
    column = lax.broadcasted_iota(jnp.int32, (1, QALL), 1)
    last_pos = total_len - LAST + ((column >> 4) * 32 + core * 16 + (column & 15)) % LAST
    key_pos = (position[0] >> 1) * tokens + lax.broadcasted_iota(jnp.int32, (tokens, QALL), 0)
    s = jnp.where(key_pos <= last_pos, s, FAR)
    scores[...] = s
    top = jnp.max(s, axis=0, keepdims=True)
    total = jnp.sum(jnp.exp(s - top), axis=0, keepdims=True)
    both = jnp.concatenate([top, total], axis=0)
    for d in range(CHIPS):
        stats[d] = both


def estimate(position, q, k_mine, k_theirs, total_len):
    return pl.pallas_call(
        functools.partial(estimate_kernel, total_len),
        out_shape=(shape(F32, 2 * k_mine.shape[0], QALL), shape(F32, CHIPS, 2, QALL)),
        in_specs=[SMEM, VMEM, VMEM, VMEM],
        out_specs=(VMEM, VMEM),
        compiler_params=SMALL,
    )(position, q, k_mine, k_theirs)


def mass_kernel(factor, stats, scores, after, out):
    tops, totals = stats[:, 0, :], stats[:, 1, :]
    top = jnp.max(tops, axis=0, keepdims=True)
    total = jnp.sum(totals * jnp.exp(tops - top), axis=0, keepdims=True)
    p = jnp.exp(scores[...] - (top + jnp.log(total)))
    kvh, local = out.shape[0] // 2, out.shape[2]
    real = (lax.broadcasted_iota(jnp.int32, (kvh, QALL), 1) < QREAL).astype(BF16)
    high = p.astype(BF16)
    low = (p - high.astype(F32)).astype(BF16)
    mass = sum(lax.dot_general(real, x, NT, preferred_element_type=F32) for x in (high, low)) * factor
    for c in range(2):
        out[c * kvh : (c + 1) * kvh, 0, :] = mass[:, c * local : (c + 1) * local]


def mass(stats, scores, after, kvh, factor):
    return pl.pallas_call(
        functools.partial(mass_kernel, factor),
        out_shape=shape(F32, 2 * kvh, 1, scores.shape[0] // 2),
        in_specs=[VMEM, VMEM, ANY],
        out_specs=VMEM,
        compiler_params=SMALL,
    )(stats, scores, after)


def block_numbers(e, slash, position):
    block = position[0] * 2 + e
    return [block] + [block - jnp.where(slash[0, j] == 0, slash[0, 0], slash[0, j]) for j in range(1, NS)]


def fetch(near, core, position, ours, theirs, k_all, v_all, sems):
    per = BLK // UNIT
    copies = []
    for j in range(NS):
        kept = jnp.where(near[j] >= 0, near[j], near[0])
        chips = (position[0] >> 1) - (kept >> 2)
        to = pl.ds(j * per, per)
        for which, target in ((0, k_all.at[to]), (1, v_all.at[to, :, pl.ds(0, HD)])):
            unit = (2 * chips + which) * 2 * per + (kept & 1) * per
            copy = pltpu.make_async_copy(ours.at[pl.ds(unit, per)], target, sems.at[len(copies)])
            other = pltpu.make_async_copy(theirs.at[pl.ds(unit, per)], target, sems.at[len(copies)])
            from_ours = ((kept >> 1) & 1) == core
            pl.when(from_ours)(copy.start)
            pl.when(jnp.logical_not(from_ours))(other.start)
            copies.append(copy)
    return copies


def fill(e, near, core, vertical, ours, theirs, k_all, v_all, copies):
    per = BLK // UNIT
    row = lax.broadcasted_iota(jnp.int32, (UNIT, HD), 0)
    drop = jnp.zeros((UNIT, HD), jnp.int32)
    for j in range(NV):
        c = vertical[0, j]
        bad = c > near[0]
        for other in near:
            bad = bad | (c == other)
        drop = jnp.where(row // PIECE == j, bad.astype(jnp.int32), drop)
    drop = drop.astype(F32)
    keep = (1.0 - drop).astype(BF16)
    first = ours[e * per, 0:1, :]
    instead = first * drop.astype(BF16)
    listed = ours.shape[0] - PIECES
    for c, (k, v) in enumerate(((ours, theirs), (theirs, ours))):

        @pl.when(core == c)
        def _(k=k, v=v):
            for i in range(PIECES):
                k_all[NEAR + i] = k[listed + i] * keep + instead
                v_all[NEAR + i, :, :HD] = v[listed + i] * keep

    for copy in copies:
        copy.wait()
    for j in range(1, NS):

        @pl.when(near[j] < 0)
        def _(j=j):
            to = slice(j * per, (j + 1) * per)
            k_all[to] = jnp.broadcast_to(first, (per, UNIT, HD))
            v_all[to, :, :HD] = jnp.zeros((per, UNIT, HD), BF16)

    counts = [jnp.where(near[j // per] >= 0, jnp.ones((UNIT, HD), F32), 0.0).astype(BF16) for j in range(NEAR)]
    return counts + [keep]


def count(v_all, counts):
    for j in range(NEAR):
        v_all[j, :, HD:] = counts[j]
    for i in range(NEAR, NEAR + PIECES):
        v_all[i, :, HD:] = counts[NEAR]


def heads(e, q_buf, o_buf, k_all, v_all, out, sems):
    factor = LOG2E / math.sqrt(HD)
    causal = lax.broadcasted_iota(jnp.int32, (BLK, BLK), 1) <= lax.broadcasted_iota(jnp.int32, (BLK, BLK), 0)
    keys = k_all[...].reshape((NV + NS) * BLK, HD)
    values = v_all[...].reshape((NV + NS) * BLK, 2 * HD)
    pair = 2
    copies = []

    def score(h):
        n = min(pair, GROUP - h)
        tile = q_buf[h : h + n].reshape(n * BLK, HD)
        s = lax.dot_general(tile, keys, NT, preferred_element_type=F32)
        own = jnp.where(jnp.concatenate([causal] * n, axis=0), s[:, :BLK], FAR)
        s = jnp.concatenate([own, s[:, BLK:]], axis=1)
        return s, jnp.max(s, axis=1, keepdims=True) * factor

    def finish(h, s, top):
        n = min(pair, GROUP - h)
        w = jnp.exp2(s * factor - top).astype(BF16)
        o = jnp.dot(w, values, preferred_element_type=F32)
        o_buf[h : h + n] = (o[:, :HD] / o[:, HD:]).astype(BF16).reshape(n, BLK, HD)
        copies.append(pltpu.make_async_copy(o_buf.at[pl.ds(h, n)], out.at[pl.ds(h, n), pl.ds(e * BLK, BLK)], sems.at[h]))
        copies[-1].start()

    held = score(0)
    for h in range(0, GROUP, pair):
        later = score(h + pair) if h + pair < GROUP else None
        finish(h, *held)
        held = later
    return copies


def first_kernel(vertical, slash, position, q, ours, theirs, out, ours_next, theirs_next, token, q_buf, o_buf, k_all, v_all, k_next, v_next, sems, near_sems, next_sems):
    token[...] = jnp.zeros_like(token)
    core = position[0] & 1
    copy = pltpu.make_async_copy(q.at[:, pl.ds(0, BLK)], q_buf, sems.at[0])
    copy.start()
    near = block_numbers(0, slash, position)
    copies = fetch(near, core, position, ours, theirs, k_all, v_all, near_sems)
    near_next = block_numbers(1, slash, position)
    copies_next = fetch(near_next, core, position, ours, theirs, k_next, v_next, next_sems)
    count(v_all, fill(0, near, core, vertical, ours, theirs, k_all, v_all, copies))
    copy.wait()
    written = heads(0, q_buf, o_buf, k_all, v_all, out, sems)
    counts = fill(1, near_next, core, vertical, ours, theirs, k_next, v_next, copies_next)
    n = NEAR + PIECES
    ours_next[:n] = k_next[...]
    theirs_next[:n] = v_next[...]
    for j, x in enumerate(counts):
        ours_next[n + j] = x
    for copy in written:
        copy.wait()


def second_kernel(q, ours, theirs, before, out, q_buf, o_buf, v_all, sems):
    n = NEAR + PIECES
    copy = pltpu.make_async_copy(q.at[:, pl.ds(BLK, BLK)], q_buf, sems.at[0])
    copy.start()
    v_all[:, :, :HD] = theirs[:n]
    count(v_all, [ours[n + j] for j in range(NEAR + 1)])
    copy.wait()
    for copy in heads(1, q_buf, o_buf, ours.at[pl.ds(0, n)], v_all, out, sems):
        copy.wait()


COST = pl.CostEstimate(flops=4 * GROUP * (NV + NS) * BLK**3, bytes_accessed=2 * 1024 * 1024, transcendentals=GROUP * (NV + NS) * BLK**2)
KEYS = (NEAR + PIECES, UNIT, HD)
VALUES = (NEAR + PIECES, UNIT, 2 * HD)
TILE = (GROUP, BLK, HD)


def attend_first(vertical, slash, position, q_t, ours, theirs):
    return pl.pallas_call(
        first_kernel,
        out_shape=(shape(BF16, *q_t.shape), shape(BF16, *ours.shape), shape(BF16, *ours.shape), shape(F32, 8, 128)),
        in_specs=[SMEM] * 3 + [HBM, VMEM, VMEM],
        out_specs=(ANY, VMEM, VMEM, VMEM),
        input_output_aliases={4: 1, 5: 2},
        scratch_shapes=[
            pltpu.VMEM(TILE, BF16),
            pltpu.VMEM(TILE, BF16),
            pltpu.VMEM(KEYS, BF16),
            pltpu.VMEM(VALUES, BF16),
            pltpu.VMEM(KEYS, BF16),
            pltpu.VMEM(KEYS, BF16),
            pltpu.SemaphoreType.DMA((GROUP,)),
            pltpu.SemaphoreType.DMA((2 * NS,)),
            pltpu.SemaphoreType.DMA((2 * NS,)),
        ],
        compiler_params=MIDDLE,
        cost_estimate=COST,
    )(vertical, slash, position, q_t, ours, theirs)


def attend_second(q_t, ours, theirs, out):
    return pl.pallas_call(
        second_kernel,
        out_shape=shape(BF16, *q_t.shape),
        in_specs=[HBM, VMEM, VMEM, ANY],
        out_specs=ANY,
        scratch_shapes=[pltpu.VMEM(TILE, BF16), pltpu.VMEM(TILE, BF16), pltpu.VMEM(VALUES, BF16), pltpu.SemaphoreType.DMA((GROUP,))],
        input_output_aliases={3: 0},
        compiler_params=MIDDLE,
        cost_estimate=COST,
    )(q_t, ours, theirs, out)


def on_device(queries, key_rows, value_rows, vertical, slash_offsets):
    local = key_rows.shape[0]
    total_len = local * NY * PER_ROW
    place = lax.axis_index(CTX).reshape(1)
    q_t = jnp.transpose(queries, (1, 0, 2))
    k, v = key_rows[:, 0], value_rows[:, 0]

    sent, kv = pack(place, q_t, k, v)
    back = lambda x, chips: lax.ppermute(x, CHIP, [(i, (i + chips) % CHIPS) for i in range(CHIPS)])
    swap = lambda x: lax.ppermute(x, "core", [(0, 1), (1, 0)])
    three, k_theirs = back(kv, 3), swap(k)
    r = exchange(sent, CTX)
    mine = exchange(pick(choose(vertical), r, three, k_theirs), ("y", "zlo"))
    one, two, four = back(kv, 1), back(three, -1), back(kv, 4)
    scores, stats = estimate(place, mine[:, LISTED:].reshape(QALL, HD), k, k_theirs, total_len)
    ours = together([kv, one, two, three, four], mine, scores)
    theirs = swap(ours)

    out, ours, theirs, token = attend_first(vertical, slash_offsets, place, q_t, ours, theirs)
    stats = exchange(stats, CHIP)
    part = exchange(mass(stats, scores, token, lax.axis_size("kvh"), total_len / LAST / HEADS), ("core", "kvh"))
    out = attend_second(q_t, ours, theirs, out)
    profile = jnp.sum(part, axis=(0, 1))
    return jnp.transpose(out, (1, 0, 2)), profile


def solution(mesh):
    wide = Mesh(mesh.devices.reshape(NY, NZ // 2, 2, 2, -1), CTX + ("kvh",))
    return jax.shard_map(
        on_device,
        mesh=wide,
        in_specs=(P(CTX, "kvh", None), P(CTX, "kvh", None), P(CTX, "kvh", None), P("kvh", None), P("kvh", None)),
        out_specs=(P(CTX, "kvh", None), P(CTX)),
        check_vma=False,
    )
```

```python
import functools
import math

import jax
import jax.numpy as jnp
from jax import lax
from jax.experimental import pallas as pl
from jax.experimental.pallas import tpu as pltpu
from jax.sharding import Mesh
from jax.sharding import PartitionSpec as P

BLK = 128
LAST = 64
NV = 16
NS = 8
HEADS = 40
HD = 128
GROUP = 5
FAR = -1e30
LOG2E = math.log2(math.e)
CHIP = ("y", "zhi", "zlo")
CTX = CHIP + ("core",)
NY, NZ = 8, 4
PER_ROW = 2 * NZ
CHIPS = NY * NZ
PIECES = CHIPS // 2
PIECE = BLK // PIECES
LISTED = NV * PIECE
UNIT = LISTED
NEAR = NS * BLK // UNIT
BACK = 5
QROWS = 16
QREAL = GROUP * LAST // 2
QALL = 256
NT = (((1,), (1,)), ((), ()))
SMEM = pl.BlockSpec(memory_space=pltpu.SMEM)
VMEM = pl.BlockSpec(memory_space=pltpu.VMEM)
ANY = pl.BlockSpec(memory_space=pl.ANY)
HBM = pl.BlockSpec(memory_space=pltpu.HBM)
F32 = jnp.float32
BF16 = jnp.bfloat16
LARGE = pltpu.CompilerParams(vmem_limit_bytes=60 * 1024 * 1024)
MIDDLE = pltpu.CompilerParams(vmem_limit_bytes=32 * 1024 * 1024)
SMALL = pltpu.CompilerParams(vmem_limit_bytes=8 * 1024 * 1024)


def shape(kind, *dims):
    return jax.ShapeDtypeStruct(dims, kind)


def exchange(x, axis):
    return lax.all_to_all(x, axis, 0, 0)


def pack_kernel(position, q, k, v, sent, kv, k_buf, v_buf, last, sems):
    local = k.shape[0]
    loads = [pltpu.make_async_copy(x, y, sems.at[i]) for i, (x, y) in enumerate(((k, k_buf), (v, v_buf), (q.at[:, pl.ds(local - LAST, LAST)], last)))]
    for copy in loads:
        copy.start()

    def spread(pieces):
        for y in range(NY):
            for zhi in range(NZ // 2):
                for zlo in range(2):
                    for c in range(2):
                        sent[((y * NZ // 2 + zhi) * 2 + zlo) * 2 + c] = pieces[c][2 * y + zlo]

    cut = []
    for which, x in enumerate((k_buf, v_buf)):
        loads[which].wait()
        kv[which * local // UNIT : (which + 1) * local // UNIT] = x[...].reshape(local // UNIT, UNIT, HD)
        x = x[...].astype(F32).reshape(2, PIECES, PIECE, HD)
        cut.append(jnp.concatenate([x[0], x[1]], axis=1).astype(BF16))
    spread(cut)
    loads[2].wait()

    @pl.when(position[0] == 2 * CHIPS - 1)
    def _():
        flat = last[...].reshape(GROUP * LAST, HD)
        flat = jnp.concatenate([flat, jnp.zeros((2 * local - GROUP * LAST, HD), BF16)], axis=0)
        flat = flat.reshape(PIECES, 2, 2 * PIECE, HD)
        spread([flat[:, 0], flat[:, 1]])


def pack(position, q_t, k, v):
    local = k.shape[0]
    return pl.pallas_call(
        pack_kernel,
        out_shape=(shape(BF16, 2 * CHIPS, 2 * PIECE, HD), shape(BF16, 2 * local // UNIT, UNIT, HD)),
        in_specs=[SMEM, ANY, ANY, ANY],
        out_specs=(VMEM, VMEM),
        scratch_shapes=[
            pltpu.VMEM(k.shape, BF16),
            pltpu.VMEM(v.shape, BF16),
            pltpu.VMEM((GROUP, LAST, HD), BF16),
            pltpu.SemaphoreType.DMA((3,)),
        ],
        compiler_params=LARGE,
    )(position, q_t, k, v)


def choose_kernel(ids, out):
    wanted, given = out.shape
    row = lax.broadcasted_iota(jnp.int32, (wanted, HD), 0)
    source = given - wanted + row
    for j in range(NV):
        source = jnp.where(row // PIECE == j, ids[0, j] * PIECE + row % PIECE, source)
    column = lax.broadcasted_iota(jnp.int32, (wanted, HD), 1)
    for i in range(0, given, HD):
        out[:, i : i + HD] = (column + i == source).astype(F32).astype(BF16)


def choose(vertical):
    return pl.pallas_call(
        choose_kernel,
        out_shape=shape(BF16, LISTED + QROWS, 4 * CHIPS * PIECE),
        in_specs=[SMEM],
        out_specs=VMEM,
        compiler_params=SMALL,
    )(vertical)


def pick_kernel(chosen, r, three, k_theirs, out):
    rows = r[...].reshape(4 * CHIPS * PIECE, HD)
    tile = jnp.dot(chosen[...], rows, preferred_element_type=F32).astype(BF16)
    for d in range(PIECES):
        out[d] = tile


def pick(chosen, r, three, k_theirs):
    return pl.pallas_call(
        pick_kernel,
        out_shape=shape(BF16, PIECES, LISTED + QROWS, HD),
        in_specs=[VMEM, VMEM, ANY, ANY],
        out_specs=VMEM,
        compiler_params=SMALL,
    )(chosen, r, three, k_theirs)


def together_kernel(*refs):
    *parts, mine, after, out, sems = refs
    n = len(parts)
    each = parts[0].shape[0]
    copies = [pltpu.make_async_copy(part, out.at[pl.ds(each * i, each)], sems.at[i]) for i, part in enumerate(parts)]
    copies.append(pltpu.make_async_copy(mine.at[:, pl.ds(0, LISTED)], out.at[pl.ds(each * n, PIECES)], sems.at[n]))
    for copy in copies:
        copy.start()
    for copy in copies:
        copy.wait()


def together(parts, mine, after):
    n = len(parts)
    return pl.pallas_call(
        together_kernel,
        out_shape=shape(BF16, n * parts[0].shape[0] + PIECES, UNIT, HD),
        in_specs=[ANY] * (n + 2),
        out_specs=ANY,
        scratch_shapes=[pltpu.SemaphoreType.DMA((n + 1,))],
        compiler_params=SMALL,
    )(*parts, mine, after)


def estimate_kernel(total_len, position, q, k_mine, k_theirs, scores, stats):
    tokens = 2 * k_mine.shape[0]
    core = position[0] & 1
    mine, theirs = k_mine[...], k_theirs[...]
    k = jnp.concatenate([jnp.where(core == 0, mine, theirs), jnp.where(core == 0, theirs, mine)], axis=0)
    s = lax.dot_general(k, q[...], NT, preferred_element_type=F32) * (1.0 / math.sqrt(HD))
    column = lax.broadcasted_iota(jnp.int32, (1, QALL), 1)
    last_pos = total_len - LAST + ((column >> 4) * 32 + core * 16 + (column & 15)) % LAST
    key_pos = (position[0] >> 1) * tokens + lax.broadcasted_iota(jnp.int32, (tokens, QALL), 0)
    s = jnp.where(key_pos <= last_pos, s, FAR)
    scores[...] = s
    top = jnp.max(s, axis=0, keepdims=True)
    total = jnp.sum(jnp.exp(s - top), axis=0, keepdims=True)
    both = jnp.concatenate([top, total], axis=0)
    for d in range(CHIPS):
        stats[d] = both


def estimate(position, q, k_mine, k_theirs, total_len):
    return pl.pallas_call(
        functools.partial(estimate_kernel, total_len),
        out_shape=(shape(F32, 2 * k_mine.shape[0], QALL), shape(F32, CHIPS, 2, QALL)),
        in_specs=[SMEM, VMEM, VMEM, VMEM],
        out_specs=(VMEM, VMEM),
        compiler_params=SMALL,
    )(position, q, k_mine, k_theirs)


def mass_kernel(factor, stats, scores, after, out):
    tops, totals = stats[:, 0, :], stats[:, 1, :]
    top = jnp.max(tops, axis=0, keepdims=True)
    total = jnp.sum(totals * jnp.exp(tops - top), axis=0, keepdims=True)
    p = jnp.exp(scores[...] - (top + jnp.log(total)))
    kvh, local = out.shape[0] // 2, out.shape[2]
    real = (lax.broadcasted_iota(jnp.int32, (kvh, QALL), 1) < QREAL).astype(BF16)
    high = p.astype(BF16)
    low = (p - high.astype(F32)).astype(BF16)
    mass = sum(lax.dot_general(real, x, NT, preferred_element_type=F32) for x in (high, low)) * factor
    for c in range(2):
        out[c * kvh : (c + 1) * kvh, 0, :] = mass[:, c * local : (c + 1) * local]


def mass(stats, scores, after, kvh, factor):
    return pl.pallas_call(
        functools.partial(mass_kernel, factor),
        out_shape=shape(F32, 2 * kvh, 1, scores.shape[0] // 2),
        in_specs=[VMEM, VMEM, ANY],
        out_specs=VMEM,
        compiler_params=SMALL,
    )(stats, scores, after)


def block_numbers(e, slash, position):
    block = position[0] * 2 + e
    return [block] + [block - jnp.where(slash[0, j] == 0, slash[0, 0], slash[0, j]) for j in range(1, NS)]


def fetch(near, core, position, ours, theirs, k_all, v_all, sems):
    per = BLK // UNIT
    copies = []
    for j in range(NS):
        kept = jnp.where(near[j] >= 0, near[j], near[0])
        chips = (position[0] >> 1) - (kept >> 2)
        to = pl.ds(j * per, per)
        for which, target in ((0, k_all.at[to]), (1, v_all.at[to, :, pl.ds(0, HD)])):
            unit = (2 * chips + which) * 2 * per + (kept & 1) * per
            copy = pltpu.make_async_copy(ours.at[pl.ds(unit, per)], target, sems.at[len(copies)])
            other = pltpu.make_async_copy(theirs.at[pl.ds(unit, per)], target, sems.at[len(copies)])
            from_ours = ((kept >> 1) & 1) == core
            pl.when(from_ours)(copy.start)
            pl.when(jnp.logical_not(from_ours))(other.start)
            copies.append(copy)
    return copies


def fill(e, near, core, vertical, ours, theirs, k_all, v_all, copies):
    per = BLK // UNIT
    row = lax.broadcasted_iota(jnp.int32, (UNIT, HD), 0)
    drop = jnp.zeros((UNIT, HD), jnp.int32)
    for j in range(NV):
        c = vertical[0, j]
        bad = c > near[0]
        for other in near:
            bad = bad | (c == other)
        drop = jnp.where(row // PIECE == j, bad.astype(jnp.int32), drop)
    drop = drop.astype(F32)
    keep = (1.0 - drop).astype(BF16)
    first = ours[e * per, 0:1, :]
    instead = first * drop.astype(BF16)
    listed = ours.shape[0] - PIECES
    for c, (k, v) in enumerate(((ours, theirs), (theirs, ours))):

        @pl.when(core == c)
        def _(k=k, v=v):
            for i in range(PIECES):
                k_all[NEAR + i] = k[listed + i] * keep + instead
                v_all[NEAR + i, :, :HD] = v[listed + i] * keep

    for copy in copies:
        copy.wait()
    for j in range(1, NS):

        @pl.when(near[j] < 0)
        def _(j=j):
            to = slice(j * per, (j + 1) * per)
            k_all[to] = jnp.broadcast_to(first, (per, UNIT, HD))
            v_all[to, :, :HD] = jnp.zeros((per, UNIT, HD), BF16)

    counts = [jnp.where(near[j // per] >= 0, jnp.ones((UNIT, HD), F32), 0.0).astype(BF16) for j in range(NEAR)]
    return counts + [keep]


def count(v_all, counts):
    for j in range(NEAR):
        v_all[j, :, HD:] = counts[j]
    for i in range(NEAR, NEAR + PIECES):
        v_all[i, :, HD:] = counts[NEAR]


def heads(e, q_buf, o_buf, k_all, v_all, out, sems):
    factor = LOG2E / math.sqrt(HD)
    causal = lax.broadcasted_iota(jnp.int32, (BLK, BLK), 1) <= lax.broadcasted_iota(jnp.int32, (BLK, BLK), 0)
    keys = k_all[...].reshape((NV + NS) * BLK, HD)
    values = v_all[...].reshape((NV + NS) * BLK, 2 * HD)
    pair = 2
    copies = []

    def score(h):
        n = min(pair, GROUP - h)
        tile = q_buf[h : h + n].reshape(n * BLK, HD)
        s = lax.dot_general(tile, keys, NT, preferred_element_type=F32)
        own = jnp.where(jnp.concatenate([causal] * n, axis=0), s[:, :BLK], FAR)
        s = jnp.concatenate([own, s[:, BLK:]], axis=1)
        return s, jnp.max(s, axis=1, keepdims=True) * factor

    def finish(h, s, top):
        n = min(pair, GROUP - h)
        w = jnp.exp2(s * factor - top).astype(BF16)
        o = jnp.dot(w, values, preferred_element_type=F32)
        o_buf[h : h + n] = (o[:, :HD] / o[:, HD:]).astype(BF16).reshape(n, BLK, HD)
        copies.append(pltpu.make_async_copy(o_buf.at[pl.ds(h, n)], out.at[pl.ds(h, n), pl.ds(e * BLK, BLK)], sems.at[h]))
        copies[-1].start()

    held = score(0)
    for h in range(0, GROUP, pair):
        later = score(h + pair) if h + pair < GROUP else None
        finish(h, *held)
        held = later
    return copies


def first_kernel(vertical, slash, position, q, ours, theirs, out, ours_next, theirs_next, token, q_buf, o_buf, k_all, v_all, k_next, v_next, sems, near_sems, next_sems):
    token[...] = jnp.zeros_like(token)
    core = position[0] & 1
    copy = pltpu.make_async_copy(q.at[:, pl.ds(0, BLK)], q_buf, sems.at[0])
    copy.start()
    near = block_numbers(0, slash, position)
    copies = fetch(near, core, position, ours, theirs, k_all, v_all, near_sems)
    near_next = block_numbers(1, slash, position)
    copies_next = fetch(near_next, core, position, ours, theirs, k_next, v_next, next_sems)
    count(v_all, fill(0, near, core, vertical, ours, theirs, k_all, v_all, copies))
    copy.wait()
    written = heads(0, q_buf, o_buf, k_all, v_all, out, sems)
    counts = fill(1, near_next, core, vertical, ours, theirs, k_next, v_next, copies_next)
    n = NEAR + PIECES
    ours_next[:n] = k_next[...]
    copy = pltpu.make_async_copy(v_next, theirs_next.at[pl.ds(0, n)], sems.at[GROUP])
    copy.start()
    for j, x in enumerate(counts):
        ours_next[n + j] = x
    for copy in written + [copy]:
        copy.wait()


def second_kernel(q, ours, theirs, before, out, q_buf, o_buf, v_all, sems):
    n = NEAR + PIECES
    copy = pltpu.make_async_copy(q.at[:, pl.ds(BLK, BLK)], q_buf, sems.at[0])
    copy.start()
    values = pltpu.make_async_copy(theirs.at[pl.ds(0, n)], v_all.at[:, :, pl.ds(0, HD)], sems.at[1])
    values.start()
    count(v_all, [ours[n + j] for j in range(NEAR + 1)])
    copy.wait()
    values.wait()
    for copy in heads(1, q_buf, o_buf, ours.at[pl.ds(0, n)], v_all, out, sems):
        copy.wait()


COST = pl.CostEstimate(flops=4 * GROUP * (NV + NS) * BLK**3, bytes_accessed=2 * 1024 * 1024, transcendentals=GROUP * (NV + NS) * BLK**2)
KEYS = (NEAR + PIECES, UNIT, HD)
VALUES = (NEAR + PIECES, UNIT, 2 * HD)
TILE = (GROUP, BLK, HD)


def attend_first(vertical, slash, position, q_t, ours, theirs):
    return pl.pallas_call(
        first_kernel,
        out_shape=(shape(BF16, *q_t.shape), shape(BF16, *ours.shape), shape(BF16, *ours.shape), shape(F32, 8, 128)),
        in_specs=[SMEM] * 3 + [HBM, VMEM, VMEM],
        out_specs=(ANY, VMEM, ANY, VMEM),
        input_output_aliases={4: 1, 5: 2},
        scratch_shapes=[
            pltpu.VMEM(TILE, BF16),
            pltpu.VMEM(TILE, BF16),
            pltpu.VMEM(KEYS, BF16),
            pltpu.VMEM(VALUES, BF16),
            pltpu.VMEM(KEYS, BF16),
            pltpu.VMEM(KEYS, BF16),
            pltpu.SemaphoreType.DMA((GROUP + 1,)),
            pltpu.SemaphoreType.DMA((2 * NS,)),
            pltpu.SemaphoreType.DMA((2 * NS,)),
        ],
        compiler_params=MIDDLE,
        cost_estimate=COST,
    )(vertical, slash, position, q_t, ours, theirs)


def attend_second(q_t, ours, theirs, out):
    return pl.pallas_call(
        second_kernel,
        out_shape=shape(BF16, *q_t.shape),
        in_specs=[HBM, VMEM, ANY, ANY],
        out_specs=ANY,
        scratch_shapes=[pltpu.VMEM(TILE, BF16), pltpu.VMEM(TILE, BF16), pltpu.VMEM(VALUES, BF16), pltpu.SemaphoreType.DMA((GROUP,))],
        input_output_aliases={3: 0},
        compiler_params=MIDDLE,
        cost_estimate=COST,
    )(q_t, ours, theirs, out)


def on_device(queries, key_rows, value_rows, vertical, slash_offsets):
    local = key_rows.shape[0]
    total_len = local * NY * PER_ROW
    place = lax.axis_index(CTX).reshape(1)
    q_t = jnp.transpose(queries, (1, 0, 2))
    k, v = key_rows[:, 0], value_rows[:, 0]

    sent, kv = pack(place, q_t, k, v)
    back = lambda x, chips: lax.ppermute(x, CHIP, [(i, (i + chips) % CHIPS) for i in range(CHIPS)])
    swap = lambda x: lax.ppermute(x, "core", [(0, 1), (1, 0)])
    three, k_theirs = back(kv, 3), swap(k)
    r = exchange(sent, CTX)
    mine = exchange(pick(choose(vertical), r, three, k_theirs), ("y", "zlo"))
    one, two, four = back(kv, 1), back(three, -1), back(kv, 4)
    scores, stats = estimate(place, mine[:, LISTED:].reshape(QALL, HD), k, k_theirs, total_len)
    ours = together([kv, one, two, three, four], mine, scores)
    theirs = swap(ours)

    out, ours, theirs, token = attend_first(vertical, slash_offsets, place, q_t, ours, theirs)
    stats = exchange(stats, CHIP)
    part = exchange(mass(stats, scores, token, lax.axis_size("kvh"), total_len / LAST / HEADS), ("core", "kvh"))
    out = attend_second(q_t, ours, theirs, out)
    profile = jnp.sum(part, axis=(0, 1))
    return jnp.transpose(out, (1, 0, 2)), profile


def solution(mesh):
    wide = Mesh(mesh.devices.reshape(NY, NZ // 2, 2, 2, -1), CTX + ("kvh",))
    return jax.shard_map(
        on_device,
        mesh=wide,
        in_specs=(P(CTX, "kvh", None), P(CTX, "kvh", None), P(CTX, "kvh", None), P("kvh", None), P("kvh", None)),
        out_specs=(P(CTX, "kvh", None), P(CTX)),
        check_vma=False,
    )
```

```python
import functools
import math

import jax
import jax.numpy as jnp
from jax import lax
from jax.experimental import pallas as pl
from jax.experimental.pallas import tpu as pltpu
from jax.sharding import Mesh
from jax.sharding import PartitionSpec as P

BLK = 128
LAST = 64
NV = 16
NS = 8
HEADS = 40
HD = 128
GROUP = 5
FAR = -1e30
LOG2E = math.log2(math.e)
CHIP = ("y", "zhi", "zlo")
CTX = CHIP + ("core",)
NY, NZ = 8, 4
PER_ROW = 2 * NZ
CHIPS = NY * NZ
PIECES = CHIPS // 2
PIECE = BLK // PIECES
LISTED = NV * PIECE
UNIT = LISTED
NEAR = NS * BLK // UNIT
BACK = 5
QROWS = 16
QREAL = GROUP * LAST // 2
QALL = 256
NT = (((1,), (1,)), ((), ()))
SMEM = pl.BlockSpec(memory_space=pltpu.SMEM)
VMEM = pl.BlockSpec(memory_space=pltpu.VMEM)
ANY = pl.BlockSpec(memory_space=pl.ANY)
HBM = pl.BlockSpec(memory_space=pltpu.HBM)
F32 = jnp.float32
BF16 = jnp.bfloat16
LARGE = pltpu.CompilerParams(vmem_limit_bytes=60 * 1024 * 1024)
MIDDLE = pltpu.CompilerParams(vmem_limit_bytes=32 * 1024 * 1024)
SMALL = pltpu.CompilerParams(vmem_limit_bytes=8 * 1024 * 1024)


def shape(kind, *dims):
    return jax.ShapeDtypeStruct(dims, kind)


def exchange(x, axis):
    return lax.all_to_all(x, axis, 0, 0)


def pack_kernel(position, q, k, v, sent, kv, k_buf, v_buf, last, sems):
    local = k.shape[0]
    loads = [pltpu.make_async_copy(x, y, sems.at[i]) for i, (x, y) in enumerate(((k, k_buf), (v, v_buf), (q.at[:, pl.ds(local - LAST, LAST)], last)))]
    for copy in loads:
        copy.start()

    def spread(pieces):
        for y in range(NY):
            for zhi in range(NZ // 2):
                for zlo in range(2):
                    for c in range(2):
                        sent[((y * NZ // 2 + zhi) * 2 + zlo) * 2 + c] = pieces[c][2 * y + zlo]

    cut = []
    for which, x in enumerate((k_buf, v_buf)):
        loads[which].wait()
        kv[which * local // UNIT : (which + 1) * local // UNIT] = x[...].reshape(local // UNIT, UNIT, HD)
        x = x[...].astype(F32).reshape(2, PIECES, PIECE, HD)
        cut.append(jnp.concatenate([x[0], x[1]], axis=1).astype(BF16))
    spread(cut)
    loads[2].wait()

    @pl.when(position[0] == 2 * CHIPS - 1)
    def _():
        flat = last[...].reshape(GROUP * LAST, HD)
        flat = jnp.concatenate([flat, jnp.zeros((2 * local - GROUP * LAST, HD), BF16)], axis=0)
        flat = flat.reshape(PIECES, 2, 2 * PIECE, HD)
        spread([flat[:, 0], flat[:, 1]])


def pack(position, q_t, k, v):
    local = k.shape[0]
    return pl.pallas_call(
        pack_kernel,
        out_shape=(shape(BF16, 2 * CHIPS, 2 * PIECE, HD), shape(BF16, 2 * local // UNIT, UNIT, HD)),
        in_specs=[SMEM, ANY, ANY, ANY],
        out_specs=(VMEM, VMEM),
        scratch_shapes=[
            pltpu.VMEM(k.shape, BF16),
            pltpu.VMEM(v.shape, BF16),
            pltpu.VMEM((GROUP, LAST, HD), BF16),
            pltpu.SemaphoreType.DMA((3,)),
        ],
        compiler_params=LARGE,
    )(position, q_t, k, v)


def choose_kernel(ids, out):
    wanted, given = out.shape
    row = lax.broadcasted_iota(jnp.int32, (wanted, HD), 0)
    source = given - wanted + row
    for j in range(NV):
        source = jnp.where(row // PIECE == j, ids[0, j] * PIECE + row % PIECE, source)
    column = lax.broadcasted_iota(jnp.int32, (wanted, HD), 1)
    for i in range(0, given, HD):
        out[:, i : i + HD] = (column + i == source).astype(F32).astype(BF16)


def choose(vertical):
    return pl.pallas_call(
        choose_kernel,
        out_shape=shape(BF16, LISTED + QROWS, 4 * CHIPS * PIECE),
        in_specs=[SMEM],
        out_specs=VMEM,
        compiler_params=SMALL,
    )(vertical)


def pick_kernel(chosen, r, three, k_theirs, out):
    rows = r[...].reshape(4 * CHIPS * PIECE, HD)
    tile = jnp.dot(chosen[...], rows, preferred_element_type=F32).astype(BF16)
    for d in range(PIECES):
        out[d] = tile


def pick(chosen, r, three, k_theirs):
    return pl.pallas_call(
        pick_kernel,
        out_shape=shape(BF16, PIECES, LISTED + QROWS, HD),
        in_specs=[VMEM, VMEM, ANY, ANY],
        out_specs=VMEM,
        compiler_params=SMALL,
    )(chosen, r, three, k_theirs)


def together_kernel(*refs):
    *parts, after, out, sems = refs
    each = parts[0].shape[0]
    copies = [pltpu.make_async_copy(part, out.at[pl.ds(each * i, each)], sems.at[i]) for i, part in enumerate(parts)]
    for copy in copies:
        copy.start()
    for copy in copies:
        copy.wait()


def together(parts, after):
    n = len(parts)
    return pl.pallas_call(
        together_kernel,
        out_shape=shape(BF16, n * parts[0].shape[0], UNIT, HD),
        in_specs=[ANY] * (n + 1),
        out_specs=ANY,
        scratch_shapes=[pltpu.SemaphoreType.DMA((n + 1,))],
        compiler_params=SMALL,
    )(*parts, after)


def estimate_kernel(total_len, position, q, k_mine, k_theirs, scores, stats):
    tokens = 2 * k_mine.shape[0]
    core = position[0] & 1
    mine, theirs = k_mine[...], k_theirs[...]
    k = jnp.concatenate([jnp.where(core == 0, mine, theirs), jnp.where(core == 0, theirs, mine)], axis=0)
    s = lax.dot_general(k, q[...], NT, preferred_element_type=F32) * (1.0 / math.sqrt(HD))
    column = lax.broadcasted_iota(jnp.int32, (1, QALL), 1)
    last_pos = total_len - LAST + ((column >> 4) * 32 + core * 16 + (column & 15)) % LAST
    key_pos = (position[0] >> 1) * tokens + lax.broadcasted_iota(jnp.int32, (tokens, QALL), 0)
    s = jnp.where(key_pos <= last_pos, s, FAR)
    scores[...] = s
    top = jnp.max(s, axis=0, keepdims=True)
    total = jnp.sum(jnp.exp(s - top), axis=0, keepdims=True)
    both = jnp.concatenate([top, total], axis=0)
    for d in range(CHIPS):
        stats[d] = both


def estimate(position, q, k_mine, k_theirs, total_len):
    return pl.pallas_call(
        functools.partial(estimate_kernel, total_len),
        out_shape=(shape(F32, 2 * k_mine.shape[0], QALL), shape(F32, CHIPS, 2, QALL)),
        in_specs=[SMEM, VMEM, VMEM, VMEM],
        out_specs=(VMEM, VMEM),
        compiler_params=SMALL,
    )(position, q, k_mine, k_theirs)


def mass_kernel(factor, stats, scores, after, out):
    tops, totals = stats[:, 0, :], stats[:, 1, :]
    top = jnp.max(tops, axis=0, keepdims=True)
    total = jnp.sum(totals * jnp.exp(tops - top), axis=0, keepdims=True)
    p = jnp.exp(scores[...] - (top + jnp.log(total)))
    kvh, local = out.shape[0] // 2, out.shape[2]
    real = (lax.broadcasted_iota(jnp.int32, (kvh, QALL), 1) < QREAL).astype(BF16)
    high = p.astype(BF16)
    low = (p - high.astype(F32)).astype(BF16)
    mass = sum(lax.dot_general(real, x, NT, preferred_element_type=F32) for x in (high, low)) * factor
    for c in range(2):
        out[c * kvh : (c + 1) * kvh, 0, :] = mass[:, c * local : (c + 1) * local]


def mass(stats, scores, after, kvh, factor):
    return pl.pallas_call(
        functools.partial(mass_kernel, factor),
        out_shape=shape(F32, 2 * kvh, 1, scores.shape[0] // 2),
        in_specs=[VMEM, VMEM, ANY],
        out_specs=VMEM,
        compiler_params=SMALL,
    )(stats, scores, after)


def block_numbers(e, slash, position):
    block = position[0] * 2 + e
    return [block] + [block - jnp.where(slash[0, j] == 0, slash[0, 0], slash[0, j]) for j in range(1, NS)]


def fetch(near, core, position, ours, theirs, k_all, v_all, sems):
    per = BLK // UNIT
    copies = []
    for j in range(NS):
        kept = jnp.where(near[j] >= 0, near[j], near[0])
        chips = (position[0] >> 1) - (kept >> 2)
        to = pl.ds(j * per, per)
        for which, target in ((0, k_all.at[to]), (1, v_all.at[to, :, pl.ds(0, HD)])):
            unit = (2 * chips + which) * 2 * per + (kept & 1) * per
            copy = pltpu.make_async_copy(ours.at[pl.ds(unit, per)], target, sems.at[len(copies)])
            other = pltpu.make_async_copy(theirs.at[pl.ds(unit, per)], target, sems.at[len(copies)])
            from_ours = ((kept >> 1) & 1) == core
            pl.when(from_ours)(copy.start)
            pl.when(jnp.logical_not(from_ours))(other.start)
            copies.append(copy)
    return copies


def fill(e, near, core, vertical, mine, theirs, own, k_all, v_all, copies):
    per = BLK // UNIT
    row = lax.broadcasted_iota(jnp.int32, (UNIT, HD), 0)
    drop = jnp.zeros((UNIT, HD), jnp.int32)
    for j in range(NV):
        c = vertical[0, j]
        bad = c > near[0]
        for other in near:
            bad = bad | (c == other)
        drop = jnp.where(row // PIECE == j, bad.astype(jnp.int32), drop)
    drop = drop.astype(F32)
    keep = (1.0 - drop).astype(BF16)
    first = own[e * per, 0:1, :]
    instead = first * drop.astype(BF16)
    for c, (k, v) in enumerate(((mine, theirs), (theirs, mine))):

        @pl.when(core == c)
        def _(k=k, v=v):
            for i in range(PIECES):
                k_all[NEAR + i] = k[i, :LISTED, :] * keep + instead
                v_all[NEAR + i, :, :HD] = v[i, :LISTED, :] * keep

    for copy in copies:
        copy.wait()
    for j in range(1, NS):

        @pl.when(near[j] < 0)
        def _(j=j):
            to = slice(j * per, (j + 1) * per)
            k_all[to] = jnp.broadcast_to(first, (per, UNIT, HD))
            v_all[to, :, :HD] = jnp.zeros((per, UNIT, HD), BF16)

    counts = [jnp.where(near[j // per] >= 0, jnp.ones((UNIT, HD), F32), 0.0).astype(BF16) for j in range(NEAR)]
    return counts + [keep]


def count(v_all, counts):
    for j in range(NEAR):
        v_all[j, :, HD:] = counts[j]
    for i in range(NEAR, NEAR + PIECES):
        v_all[i, :, HD:] = counts[NEAR]


def heads(e, q_buf, o_buf, k_all, v_all, out, sems):
    factor = LOG2E / math.sqrt(HD)
    causal = lax.broadcasted_iota(jnp.int32, (BLK, BLK), 1) <= lax.broadcasted_iota(jnp.int32, (BLK, BLK), 0)
    keys = k_all[...].reshape((NV + NS) * BLK, HD)
    values = v_all[...].reshape((NV + NS) * BLK, 2 * HD)
    pair = 2
    copies = []

    def score(h):
        n = min(pair, GROUP - h)
        tile = q_buf[h : h + n].reshape(n * BLK, HD)
        s = lax.dot_general(tile, keys, NT, preferred_element_type=F32)
        own = jnp.where(jnp.concatenate([causal] * n, axis=0), s[:, :BLK], FAR)
        s = jnp.concatenate([own, s[:, BLK:]], axis=1)
        return s, jnp.max(s, axis=1, keepdims=True) * factor

    def finish(h, s, top):
        n = min(pair, GROUP - h)
        w = jnp.exp2(s * factor - top).astype(BF16)
        o = jnp.dot(w, values, preferred_element_type=F32)
        o_buf[h : h + n] = (o[:, :HD] / o[:, HD:]).astype(BF16).reshape(n, BLK, HD)
        copies.append(pltpu.make_async_copy(o_buf.at[pl.ds(h, n)], out.at[pl.ds(h, n), pl.ds(e * BLK, BLK)], sems.at[h]))
        copies[-1].start()

    held = score(0)
    for h in range(0, GROUP, pair):
        later = score(h + pair) if h + pair < GROUP else None
        finish(h, *held)
        held = later
    return copies


def handed_on(k, v, u, mine, theirs, near_mine, near_theirs):
    near, far, rows = pl.ds(0, NEAR), pl.ds(NEAR, PIECES), pl.ds(0, LISTED)
    left = pl.ds(0, HD)
    return (
        (k.at[near], near_mine.at[near]),
        (k.at[far], mine.at[:, rows]),
        (v.at[near, :, left], near_theirs.at[near]),
        (v.at[far, :, left], theirs.at[:, rows]),
        (u, near_mine.at[pl.ds(NEAR, NEAR + 1)]),
    )


def first_kernel(vertical, slash, position, q, mine, theirs, near_mine, near_theirs, *rest):
    out, *places, token, q_buf, o_buf, k_all, v_all, k_next, v_next, u_next, sems, near_sems, next_sems = rest
    token[...] = jnp.zeros_like(token)
    core = position[0] & 1
    copy = pltpu.make_async_copy(q.at[:, pl.ds(0, BLK)], q_buf, sems.at[0])
    copy.start()
    near = block_numbers(0, slash, position)
    copies = fetch(near, core, position, near_mine, near_theirs, k_all, v_all, near_sems)
    near_next = block_numbers(1, slash, position)
    copies_next = fetch(near_next, core, position, near_mine, near_theirs, k_next, v_next, next_sems)
    count(v_all, fill(0, near, core, vertical, mine, theirs, near_mine, k_all, v_all, copies))
    copy.wait()
    written = heads(0, q_buf, o_buf, k_all, v_all, out, sems)
    for j, x in enumerate(fill(1, near_next, core, vertical, mine, theirs, near_mine, k_next, v_next, copies_next)):
        u_next[j] = x
    for i, (source, target) in enumerate(handed_on(k_next, v_next, u_next, *places)):
        written.append(pltpu.make_async_copy(source, target, sems.at[GROUP + i]))
        written[-1].start()
    for copy in written:
        copy.wait()


def second_kernel(q, mine, theirs, near_mine, near_theirs, before, out, q_buf, o_buf, k_all, v_all, u, sems):
    copies = [pltpu.make_async_copy(q.at[:, pl.ds(BLK, BLK)], q_buf, sems.at[0])]
    for i, (target, source) in enumerate(handed_on(k_all, v_all, u, mine, theirs, near_mine, near_theirs)):
        copies.append(pltpu.make_async_copy(source, target, sems.at[GROUP + i]))
    for copy in copies:
        copy.start()
    for copy in copies:
        copy.wait()
    count(v_all, [u[j] for j in range(NEAR + 1)])
    for copy in heads(1, q_buf, o_buf, k_all, v_all, out, sems):
        copy.wait()


COST = pl.CostEstimate(flops=4 * GROUP * (NV + NS) * BLK**3, bytes_accessed=2 * 1024 * 1024, transcendentals=GROUP * (NV + NS) * BLK**2)
KEYS = (NEAR + PIECES, UNIT, HD)
VALUES = (NEAR + PIECES, UNIT, 2 * HD)
COUNTS = (NEAR + 1, UNIT, HD)
TILE = (GROUP, BLK, HD)


def attend_first(vertical, slash, position, q_t, *given):
    return pl.pallas_call(
        first_kernel,
        out_shape=(shape(BF16, *q_t.shape), *(shape(BF16, *x.shape) for x in given), shape(F32, 8, 128)),
        in_specs=[SMEM] * 3 + [HBM] + [VMEM] * 4,
        out_specs=(ANY, ANY, ANY, ANY, ANY, VMEM),
        input_output_aliases={4 + i: 1 + i for i in range(4)},
        scratch_shapes=[
            pltpu.VMEM(TILE, BF16),
            pltpu.VMEM(TILE, BF16),
            pltpu.VMEM(KEYS, BF16),
            pltpu.VMEM(VALUES, BF16),
            pltpu.VMEM(KEYS, BF16),
            pltpu.VMEM(VALUES, BF16),
            pltpu.VMEM(COUNTS, BF16),
            pltpu.SemaphoreType.DMA((GROUP + 5,)),
            pltpu.SemaphoreType.DMA((2 * NS,)),
            pltpu.SemaphoreType.DMA((2 * NS,)),
        ],
        compiler_params=MIDDLE,
        cost_estimate=COST,
    )(vertical, slash, position, q_t, *given)


def attend_second(q_t, *given):
    return pl.pallas_call(
        second_kernel,
        out_shape=shape(BF16, *q_t.shape),
        in_specs=[HBM] + [ANY] * 5,
        out_specs=ANY,
        scratch_shapes=[
            pltpu.VMEM(TILE, BF16),
            pltpu.VMEM(TILE, BF16),
            pltpu.VMEM(KEYS, BF16),
            pltpu.VMEM(VALUES, BF16),
            pltpu.VMEM(COUNTS, BF16),
            pltpu.SemaphoreType.DMA((GROUP + 5,)),
        ],
        input_output_aliases={5: 0},
        compiler_params=MIDDLE,
        cost_estimate=COST,
    )(q_t, *given)


def on_device(queries, key_rows, value_rows, vertical, slash_offsets):
    local = key_rows.shape[0]
    total_len = local * NY * PER_ROW
    place = lax.axis_index(CTX).reshape(1)
    q_t = jnp.transpose(queries, (1, 0, 2))
    k, v = key_rows[:, 0], value_rows[:, 0]

    sent, kv = pack(place, q_t, k, v)
    back = lambda x, chips: lax.ppermute(x, CHIP, [(i, (i + chips) % CHIPS) for i in range(CHIPS)])
    swap = lambda x: lax.ppermute(x, "core", [(0, 1), (1, 0)])
    three, k_theirs = back(kv, 3), swap(k)
    r = exchange(sent, CTX)
    mine = exchange(pick(choose(vertical), r, three, k_theirs), ("y", "zlo"))
    one, two, four = back(kv, 1), back(three, -1), back(kv, 4)
    scores, stats = estimate(place, mine[:, LISTED:].reshape(QALL, HD), k, k_theirs, total_len)
    theirs = swap(mine)
    near_mine = together([kv, one, two, three, four], scores)
    near_theirs = swap(near_mine)

    out, *handed, token = attend_first(vertical, slash_offsets, place, q_t, mine, theirs, near_mine, near_theirs)
    stats = exchange(stats, CHIP)
    part = exchange(mass(stats, scores, token, lax.axis_size("kvh"), total_len / LAST / HEADS), ("core", "kvh"))
    out = attend_second(q_t, *handed, out)
    profile = jnp.sum(part, axis=(0, 1))
    return jnp.transpose(out, (1, 0, 2)), profile


def solution(mesh):
    wide = Mesh(mesh.devices.reshape(NY, NZ // 2, 2, 2, -1), CTX + ("kvh",))
    return jax.shard_map(
        on_device,
        mesh=wide,
        in_specs=(P(CTX, "kvh", None), P(CTX, "kvh", None), P(CTX, "kvh", None), P("kvh", None), P("kvh", None)),
        out_specs=(P(CTX, "kvh", None), P(CTX)),
        check_vma=False,
    )
```

```python
import functools
import math

import jax
import jax.numpy as jnp
from jax import lax
from jax.experimental import pallas as pl
from jax.experimental.pallas import tpu as pltpu
from jax.sharding import Mesh
from jax.sharding import PartitionSpec as P

BLK = 128
LAST = 64
NV = 16
NS = 8
HEADS = 40
HD = 128
GROUP = 5
FAR = -1e30
LOG2E = math.log2(math.e)
CHIP = ("y", "zhi", "zlo")
CTX = CHIP + ("core",)
NY, NZ = 8, 4
PER_ROW = 2 * NZ
CHIPS = NY * NZ
PIECES = CHIPS // 2
PIECE = BLK // PIECES
LISTED = NV * PIECE
UNIT = LISTED
NEAR = NS * BLK // UNIT
BACK = 5
QROWS = 16
QREAL = GROUP * LAST // 2
QALL = 256
NT = (((1,), (1,)), ((), ()))
SMEM = pl.BlockSpec(memory_space=pltpu.SMEM)
VMEM = pl.BlockSpec(memory_space=pltpu.VMEM)
ANY = pl.BlockSpec(memory_space=pl.ANY)
HBM = pl.BlockSpec(memory_space=pltpu.HBM)
F32 = jnp.float32
BF16 = jnp.bfloat16
LARGE = pltpu.CompilerParams(vmem_limit_bytes=60 * 1024 * 1024)
MIDDLE = pltpu.CompilerParams(vmem_limit_bytes=32 * 1024 * 1024)
SMALL = pltpu.CompilerParams(vmem_limit_bytes=8 * 1024 * 1024)


def shape(kind, *dims):
    return jax.ShapeDtypeStruct(dims, kind)


def exchange(x, axis):
    return lax.all_to_all(x, axis, 0, 0)


def pack_kernel(position, q, k, v, sent, kv, k_buf, v_buf, last, sems):
    local = k.shape[0]
    loads = [pltpu.make_async_copy(x, y, sems.at[i]) for i, (x, y) in enumerate(((k, k_buf), (v, v_buf), (q.at[:, pl.ds(local - LAST, LAST)], last)))]
    for copy in loads:
        copy.start()

    def spread(pieces):
        for y in range(NY):
            for zhi in range(NZ // 2):
                for zlo in range(2):
                    for c in range(2):
                        sent[((y * NZ // 2 + zhi) * 2 + zlo) * 2 + c] = pieces[c][2 * y + zlo]

    cut = []
    for which, x in enumerate((k_buf, v_buf)):
        loads[which].wait()
        kv[which * local // UNIT : (which + 1) * local // UNIT] = x[...].reshape(local // UNIT, UNIT, HD)
        x = x[...].astype(F32).reshape(2, PIECES, PIECE, HD)
        cut.append(jnp.concatenate([x[0], x[1]], axis=1).astype(BF16))
    spread(cut)
    loads[2].wait()

    @pl.when(position[0] == 2 * CHIPS - 1)
    def _():
        flat = last[...].reshape(GROUP * LAST, HD)
        flat = jnp.concatenate([flat, jnp.zeros((2 * local - GROUP * LAST, HD), BF16)], axis=0)
        flat = flat.reshape(PIECES, 2, 2 * PIECE, HD)
        spread([flat[:, 0], flat[:, 1]])


def pack(position, q_t, k, v):
    local = k.shape[0]
    return pl.pallas_call(
        pack_kernel,
        out_shape=(shape(BF16, 2 * CHIPS, 2 * PIECE, HD), shape(BF16, 2 * local // UNIT, UNIT, HD)),
        in_specs=[SMEM, ANY, ANY, ANY],
        out_specs=(VMEM, VMEM),
        scratch_shapes=[
            pltpu.VMEM(k.shape, BF16),
            pltpu.VMEM(v.shape, BF16),
            pltpu.VMEM((GROUP, LAST, HD), BF16),
            pltpu.SemaphoreType.DMA((3,)),
        ],
        compiler_params=LARGE,
    )(position, q_t, k, v)


def choose_kernel(ids, out):
    wanted, given = out.shape
    row = lax.broadcasted_iota(jnp.int32, (wanted, HD), 0)
    source = given - wanted + row
    for j in range(NV):
        source = jnp.where(row // PIECE == j, ids[0, j] * PIECE + row % PIECE, source)
    column = lax.broadcasted_iota(jnp.int32, (wanted, HD), 1)
    for i in range(0, given, HD):
        out[:, i : i + HD] = (column + i == source).astype(F32).astype(BF16)


def choose(vertical):
    return pl.pallas_call(
        choose_kernel,
        out_shape=shape(BF16, LISTED + QROWS, 4 * CHIPS * PIECE),
        in_specs=[SMEM],
        out_specs=VMEM,
        compiler_params=SMALL,
    )(vertical)


def pick_kernel(chosen, r, three, k_theirs, out):
    rows = r[...].reshape(4 * CHIPS * PIECE, HD)
    tile = jnp.dot(chosen[...], rows, preferred_element_type=F32).astype(BF16)
    for d in range(PIECES):
        out[d] = tile


def pick(chosen, r, three, k_theirs):
    return pl.pallas_call(
        pick_kernel,
        out_shape=shape(BF16, PIECES, LISTED + QROWS, HD),
        in_specs=[VMEM, VMEM, ANY, ANY],
        out_specs=VMEM,
        compiler_params=SMALL,
    )(chosen, r, three, k_theirs)


def together_kernel(*refs):
    *parts, _, _, out, sems = refs
    each = parts[0].shape[0]
    copies = [pltpu.make_async_copy(part, out.at[pl.ds(each * i, each)], sems.at[i]) for i, part in enumerate(parts)]
    for copy in copies:
        copy.start()
    for copy in copies:
        copy.wait()


def together(parts, *after):
    n = len(parts)
    return pl.pallas_call(
        together_kernel,
        out_shape=shape(BF16, n * parts[0].shape[0], UNIT, HD),
        in_specs=[ANY] * (n + len(after)),
        out_specs=ANY,
        scratch_shapes=[pltpu.SemaphoreType.DMA((n + 1,))],
        compiler_params=SMALL,
    )(*parts, *after)


def estimate_kernel(total_len, position, q, k_mine, k_theirs, scores, stats):
    tokens = 2 * k_mine.shape[0]
    core = position[0] & 1
    mine, theirs = k_mine[...], k_theirs[...]
    k = jnp.concatenate([jnp.where(core == 0, mine, theirs), jnp.where(core == 0, theirs, mine)], axis=0)
    s = lax.dot_general(k, q[...], NT, preferred_element_type=F32) * (1.0 / math.sqrt(HD))
    column = lax.broadcasted_iota(jnp.int32, (1, QALL), 1)
    last_pos = total_len - LAST + ((column >> 4) * 32 + core * 16 + (column & 15)) % LAST
    key_pos = (position[0] >> 1) * tokens + lax.broadcasted_iota(jnp.int32, (tokens, QALL), 0)
    s = jnp.where(key_pos <= last_pos, s, FAR)
    scores[...] = s
    top = jnp.max(s, axis=0, keepdims=True)
    total = jnp.sum(jnp.exp(s - top), axis=0, keepdims=True)
    both = jnp.concatenate([top, total], axis=0)
    for d in range(CHIPS):
        stats[d] = both


def estimate(position, q, k_mine, k_theirs, total_len):
    return pl.pallas_call(
        functools.partial(estimate_kernel, total_len),
        out_shape=(shape(F32, 2 * k_mine.shape[0], QALL), shape(F32, CHIPS, 2, QALL)),
        in_specs=[SMEM, VMEM, VMEM, VMEM],
        out_specs=(VMEM, VMEM),
        compiler_params=SMALL,
    )(position, q, k_mine, k_theirs)


def mass_kernel(factor, stats, scores, after, out):
    tops, totals = stats[:, 0, :], stats[:, 1, :]
    top = jnp.max(tops, axis=0, keepdims=True)
    total = jnp.sum(totals * jnp.exp(tops - top), axis=0, keepdims=True)
    p = jnp.exp(scores[...] - (top + jnp.log(total)))
    kvh, local = out.shape[0] // 2, out.shape[2]
    real = (lax.broadcasted_iota(jnp.int32, (kvh, QALL), 1) < QREAL).astype(BF16)
    high = p.astype(BF16)
    low = (p - high.astype(F32)).astype(BF16)
    mass = sum(lax.dot_general(real, x, NT, preferred_element_type=F32) for x in (high, low)) * factor
    for c in range(2):
        out[c * kvh : (c + 1) * kvh, 0, :] = mass[:, c * local : (c + 1) * local]


def mass(stats, scores, after, kvh, factor):
    return pl.pallas_call(
        functools.partial(mass_kernel, factor),
        out_shape=shape(F32, 2 * kvh, 1, scores.shape[0] // 2),
        in_specs=[VMEM, VMEM, ANY],
        out_specs=VMEM,
        compiler_params=SMALL,
    )(stats, scores, after)


def block_numbers(e, slash, position):
    block = position[0] * 2 + e
    return [block] + [block - jnp.where(slash[0, j] == 0, slash[0, 0], slash[0, j]) for j in range(1, NS)]


def fetch(near, core, position, ours, theirs, k_all, v_all, sems):
    per = BLK // UNIT
    copies = []
    for j in range(NS):
        kept = jnp.where(near[j] >= 0, near[j], near[0])
        chips = (position[0] >> 1) - (kept >> 2)
        to = pl.ds(j * per, per)
        for which, target in ((0, k_all.at[to]), (1, v_all.at[to, :, pl.ds(0, HD)])):
            unit = (2 * chips + which) * 2 * per + (kept & 1) * per
            copy = pltpu.make_async_copy(ours.at[pl.ds(unit, per)], target, sems.at[len(copies)])
            other = pltpu.make_async_copy(theirs.at[pl.ds(unit, per)], target, sems.at[len(copies)])
            from_ours = ((kept >> 1) & 1) == core
            pl.when(from_ours)(copy.start)
            pl.when(jnp.logical_not(from_ours))(other.start)
            copies.append(copy)
    return copies


def fill(e, near, core, vertical, mine, theirs, own, k_all, v_all, copies):
    per = BLK // UNIT
    row = lax.broadcasted_iota(jnp.int32, (UNIT, HD), 0)
    drop = jnp.zeros((UNIT, HD), jnp.int32)
    for j in range(NV):
        c = vertical[0, j]
        bad = c > near[0]
        for other in near:
            bad = bad | (c == other)
        drop = jnp.where(row // PIECE == j, bad.astype(jnp.int32), drop)
    drop = drop.astype(F32)
    keep = (1.0 - drop).astype(BF16)
    first = own[e * per, 0:1, :]
    instead = first * drop.astype(BF16)
    for c, (k, v) in enumerate(((mine, theirs), (theirs, mine))):

        @pl.when(core == c)
        def _(k=k, v=v):
            for i in range(PIECES):
                k_all[NEAR + i] = k[i, :LISTED, :] * keep + instead
                v_all[NEAR + i, :, :HD] = v[i, :LISTED, :] * keep

    for copy in copies:
        copy.wait()
    for j in range(1, NS):

        @pl.when(near[j] < 0)
        def _(j=j):
            to = slice(j * per, (j + 1) * per)
            k_all[to] = jnp.broadcast_to(first, (per, UNIT, HD))
            v_all[to, :, :HD] = jnp.zeros((per, UNIT, HD), BF16)

    counts = [jnp.where(near[j // per] >= 0, jnp.ones((UNIT, HD), F32), 0.0).astype(BF16) for j in range(NEAR)]
    return counts + [keep]


def count(v_all, counts):
    for j in range(NEAR):
        v_all[j, :, HD:] = counts[j]
    for i in range(NEAR, NEAR + PIECES):
        v_all[i, :, HD:] = counts[NEAR]


def heads(e, q_buf, o_buf, k_all, v_all, out, sems):
    factor = LOG2E / math.sqrt(HD)
    causal = lax.broadcasted_iota(jnp.int32, (BLK, BLK), 1) <= lax.broadcasted_iota(jnp.int32, (BLK, BLK), 0)
    keys = k_all[...].reshape((NV + NS) * BLK, HD)
    values = v_all[...].reshape((NV + NS) * BLK, 2 * HD)
    pair = 2
    copies = []

    def score(h):
        n = min(pair, GROUP - h)
        tile = q_buf[h : h + n].reshape(n * BLK, HD)
        s = lax.dot_general(tile, keys, NT, preferred_element_type=F32)
        own = jnp.where(jnp.concatenate([causal] * n, axis=0), s[:, :BLK], FAR)
        s = jnp.concatenate([own, s[:, BLK:]], axis=1)
        return s, jnp.max(s, axis=1, keepdims=True) * factor

    def finish(h, s, top):
        n = min(pair, GROUP - h)
        w = jnp.exp2(s * factor - top).astype(BF16)
        o = jnp.dot(w, values, preferred_element_type=F32)
        o_buf[h : h + n] = (o[:, :HD] / o[:, HD:]).astype(BF16).reshape(n, BLK, HD)
        copies.append(pltpu.make_async_copy(o_buf.at[pl.ds(h, n)], out.at[pl.ds(h, n), pl.ds(e * BLK, BLK)], sems.at[h]))
        copies[-1].start()

    held = score(0)
    for h in range(0, GROUP, pair):
        later = score(h + pair) if h + pair < GROUP else None
        finish(h, *held)
        held = later
    return copies


def handed_on(k, v, u, mine, theirs, near_mine, near_theirs):
    near, far, rows = pl.ds(0, NEAR), pl.ds(NEAR, PIECES), pl.ds(0, LISTED)
    left = pl.ds(0, HD)
    return (
        (k.at[near], near_mine.at[near]),
        (k.at[far], mine.at[:, rows]),
        (v.at[near, :, left], near_theirs.at[near]),
        (v.at[far, :, left], theirs.at[:, rows]),
        (u, near_mine.at[pl.ds(NEAR, NEAR + 1)]),
    )


def first_kernel(vertical, slash, position, q, mine, theirs, near_mine, near_theirs, *rest):
    out, *places, token, q_buf, o_buf, k_all, v_all, k_next, v_next, u_next, sems, near_sems, next_sems = rest
    token[...] = jnp.zeros_like(token)
    core = position[0] & 1
    copy = pltpu.make_async_copy(q.at[:, pl.ds(0, BLK)], q_buf, sems.at[0])
    copy.start()
    near = block_numbers(0, slash, position)
    copies = fetch(near, core, position, near_mine, near_theirs, k_all, v_all, near_sems)
    near_next = block_numbers(1, slash, position)
    copies_next = fetch(near_next, core, position, near_mine, near_theirs, k_next, v_next, next_sems)
    count(v_all, fill(0, near, core, vertical, mine, theirs, near_mine, k_all, v_all, copies))
    copy.wait()
    written = heads(0, q_buf, o_buf, k_all, v_all, out, sems)
    for j, x in enumerate(fill(1, near_next, core, vertical, mine, theirs, near_mine, k_next, v_next, copies_next)):
        u_next[j] = x
    for i, (source, target) in enumerate(handed_on(k_next, v_next, u_next, *places)):
        written.append(pltpu.make_async_copy(source, target, sems.at[GROUP + i]))
        written[-1].start()
    for copy in written:
        copy.wait()


def second_kernel(q, mine, theirs, near_mine, near_theirs, before, out, q_buf, o_buf, k_all, v_all, u, sems):
    copies = [pltpu.make_async_copy(q.at[:, pl.ds(BLK, BLK)], q_buf, sems.at[0])]
    for i, (target, source) in enumerate(handed_on(k_all, v_all, u, mine, theirs, near_mine, near_theirs)):
        copies.append(pltpu.make_async_copy(source, target, sems.at[GROUP + i]))
    for copy in copies:
        copy.start()
    for copy in copies:
        copy.wait()
    count(v_all, [u[j] for j in range(NEAR + 1)])
    for copy in heads(1, q_buf, o_buf, k_all, v_all, out, sems):
        copy.wait()


COST = pl.CostEstimate(flops=4 * GROUP * (NV + NS) * BLK**3, bytes_accessed=2 * 1024 * 1024, transcendentals=GROUP * (NV + NS) * BLK**2)
KEYS = (NEAR + PIECES, UNIT, HD)
VALUES = (NEAR + PIECES, UNIT, 2 * HD)
COUNTS = (NEAR + 1, UNIT, HD)
TILE = (GROUP, BLK, HD)


def attend_first(vertical, slash, position, q_t, *given):
    return pl.pallas_call(
        first_kernel,
        out_shape=(shape(BF16, *q_t.shape), *(shape(BF16, *x.shape) for x in given), shape(F32, 8, 128)),
        in_specs=[SMEM] * 3 + [HBM] + [VMEM] * 4,
        out_specs=(ANY, ANY, ANY, ANY, ANY, VMEM),
        input_output_aliases={4 + i: 1 + i for i in range(4)},
        scratch_shapes=[
            pltpu.VMEM(TILE, BF16),
            pltpu.VMEM(TILE, BF16),
            pltpu.VMEM(KEYS, BF16),
            pltpu.VMEM(VALUES, BF16),
            pltpu.VMEM(KEYS, BF16),
            pltpu.VMEM(VALUES, BF16),
            pltpu.VMEM(COUNTS, BF16),
            pltpu.SemaphoreType.DMA((GROUP + 5,)),
            pltpu.SemaphoreType.DMA((2 * NS,)),
            pltpu.SemaphoreType.DMA((2 * NS,)),
        ],
        compiler_params=MIDDLE,
        cost_estimate=COST,
    )(vertical, slash, position, q_t, *given)


def attend_second(q_t, *given):
    return pl.pallas_call(
        second_kernel,
        out_shape=shape(BF16, *q_t.shape),
        in_specs=[HBM] + [ANY] * 5,
        out_specs=ANY,
        scratch_shapes=[
            pltpu.VMEM(TILE, BF16),
            pltpu.VMEM(TILE, BF16),
            pltpu.VMEM(KEYS, BF16),
            pltpu.VMEM(VALUES, BF16),
            pltpu.VMEM(COUNTS, BF16),
            pltpu.SemaphoreType.DMA((GROUP + 5,)),
        ],
        input_output_aliases={5: 0},
        compiler_params=MIDDLE,
        cost_estimate=COST,
    )(q_t, *given)


def on_device(queries, key_rows, value_rows, vertical, slash_offsets):
    local = key_rows.shape[0]
    total_len = local * NY * PER_ROW
    place = lax.axis_index(CTX).reshape(1)
    q_t = jnp.transpose(queries, (1, 0, 2))
    k, v = key_rows[:, 0], value_rows[:, 0]

    sent, kv = pack(place, q_t, k, v)
    back = lambda x, chips: lax.ppermute(x, CHIP, [(i, (i + chips) % CHIPS) for i in range(CHIPS)])
    swap = lambda x: lax.ppermute(x, "core", [(0, 1), (1, 0)])
    three, k_theirs = back(kv, 3), swap(k)
    r = exchange(sent, CTX)
    mine = exchange(pick(choose(vertical), r, three, k_theirs), ("y", "zlo"))
    one, two, four = back(kv, 1), back(three, -1), back(kv, 4)
    scores, stats = estimate(place, mine[:, LISTED:].reshape(QALL, HD), k, k_theirs, total_len)
    theirs = swap(mine)
    near_mine = together([kv, one, two, three, four], scores, theirs)
    near_theirs = swap(near_mine)

    out, *handed, token = attend_first(vertical, slash_offsets, place, q_t, mine, theirs, near_mine, near_theirs)
    stats = exchange(stats, CHIP)
    part = exchange(mass(stats, scores, token, lax.axis_size("kvh"), total_len / LAST / HEADS), ("core", "kvh"))
    out = attend_second(q_t, *handed, out)
    profile = jnp.sum(part, axis=(0, 1))
    return jnp.transpose(out, (1, 0, 2)), profile


def solution(mesh):
    wide = Mesh(mesh.devices.reshape(NY, NZ // 2, 2, 2, -1), CTX + ("kvh",))
    return jax.shard_map(
        on_device,
        mesh=wide,
        in_specs=(P(CTX, "kvh", None), P(CTX, "kvh", None), P(CTX, "kvh", None), P("kvh", None), P("kvh", None)),
        out_specs=(P(CTX, "kvh", None), P(CTX)),
        check_vma=False,
    )
```
